256 devices in a mesh: grp: 8 (over z), lat: 32 (over y, x, core).
Axes of the slice: x: 4, y: 4, z: 8, core: 2. Of those that a mesh axis runs over, the one named last changes fastest.
Arguments:
- state: bfloat16 [16, 512, 4096], P(None, ('grp', 'lat')), may hold values from -6 to 6
- dep_row: int32 [512, 4096], P(('grp', 'lat')), may hold values from 0 to 510, as said below
- dep_col: int32 [512, 4096], P(('grp', 'lat')), may hold values from 0 to 4095, as said below
- row_weight: float32 [512, 4096], P(('grp', 'lat')), may hold values from 0 to 1
- col_weight: float32 [512, 4096], P(('grp', 'lat')), may hold values from 0 to 1
- wave_of: int32 [1024], replicated, may hold values from 0 to 1023, as said below
- legendre: bfloat16 [1024, 2, 256, 512], P(('grp', 'lat')), as said below
- gamma: float32 [16], replicated, may hold values from 0.3 to 30
- rad_place: int32 [256, 1024], P(('grp', 'lat')), may hold values from 0 to 32767, as said below
- optics: bfloat16 [262144, 16], P(('grp', 'lat')), may hold values from 0.049804688 to 2
- kabs: float32 [16, 128], replicated, may hold values from 0.02 to 0.3
- planck_weight: float32 [16, 128], replicated, may hold values from -1.5 to 1.5
- kdown: float32 [128, 16], replicated, may hold values from -0.5 to 0.5
Outputs:
- new_state: bfloat16 [16, 512, 4096], P(None, ('grp', 'lat'))
The draws below stay inside these ranges and needn't reach their ends.
Inputs may be any that keep to these rules, and one draw needn't show every extreme that they name: dep_row[i, j] lies between i - 2 and i + 1. (dep_col[i, j] - j) mod 4096 is one of 0, 1, 2, 4094, 4095. `wave_of`: every wavenumber once; slots 4 d to 4 d + 3 hold pairs m, 1023 - m for wavenumbers m below 512. `rad_place`: a value is owner * 1024 + slot with owner below 32 and slot below 1024; within the coarse rows of one group of 32 devices every value appears once; the 1024 coarse columns of one device's rows name one owner at most 48 times, and some device names some owner exactly 48 times. `legendre`: zero where 2 h + p exceeds 1023 minus the slot's wavenumber.
All inputs are finite; a program needn't handle non-finite values.
Results may differ from the reference program's by a relative error of at most 0.0078.
Values may be sent and summed in bfloat16 or wider, within the bound.
A program may use at most 128 MiB of HBM per device.

```python
import math
import jax
import jax.numpy as jnp
from jax import lax

NLON = 4096
LEV = 16
ROWS_DEV = 2
GPTS = 128
M_DEV = 4
DEVS = 256
NLAT = 512
M = 1024
TRUNC = 1023
NDEG2 = 512
OWNERS = 32
GROUPS = 8
CPD = 1024


def wave_map(key):
    wave_key = jax.random.fold_in(key, 101)
    pairs = jax.random.permutation(wave_key, M // 2).astype(jnp.int32).reshape(M // M_DEV, M_DEV // 2)
    partners = M - 1 - pairs
    return jnp.stack([pairs, partners], axis=2).reshape(M).astype(jnp.int32)


def draw_wave_of(key, part):
    return wave_map(key)


def draw_legendre(key, part):
    waves = wave_map(key)
    key = jax.random.fold_in(key, 7)
    shape = (M, 2, NLAT // 2, M // 2)
    values = jax.random.normal(key, shape, jnp.float32)
    half_steps = jnp.arange(M // 2, dtype=jnp.int32)
    parity = jnp.arange(2, dtype=jnp.int32)
    degree = 2 * half_steps[None, :] + parity[:, None]
    keep = (degree[None, :, :] <= (TRUNC - waves)[:, None, None]).astype(jnp.float32)
    return (values * keep[:, :, None, :] * NLAT ** (-0.5)).astype(jnp.bfloat16)


def draw_dep_row(key, part):
    key = jax.random.fold_in(key, 3)
    row_index = jnp.broadcast_to(jnp.arange(NLAT, dtype=jnp.int32)[:, None], (NLAT, NLON))
    offsets = jax.random.randint(key, (NLAT, NLON), -2, 2, dtype=jnp.int32)
    return jnp.clip(row_index + offsets, 0, NLAT - 2).astype(jnp.int32)


def draw_dep_col(key, part):
    key = jax.random.fold_in(key, 11)
    lon_index = jnp.broadcast_to(jnp.arange(NLON, dtype=jnp.int32)[None, :], (NLAT, NLON))
    offsets = jax.random.randint(key, (NLAT, NLON), -2, 3, dtype=jnp.int32)
    return ((lon_index + offsets + NLON) % NLON).astype(jnp.int32)


def draw_rad_place(key, part):
    key = jax.random.fold_in(key, 5)
    base = CPD // OWNERS
    half = base // 2

    def one_group(group_key):
        key_order, key_amount, key_slots, key_points = jax.random.split(group_key, 4)
        order = jax.random.permutation(key_order, OWNERS).astype(jnp.int32)
        amount = jax.random.randint(key_amount, (OWNERS // 2,), 0, half + 1, dtype=jnp.int32).at[0].set(half)
        shifts = jnp.zeros((OWNERS,), jnp.int32).at[order[0::2]].set(amount).at[order[1::2]].set(-amount)
        quota = base + shifts
        source_ids = jnp.arange(OWNERS, dtype=jnp.int32)[:, None]
        owner_ids = jnp.arange(OWNERS, dtype=jnp.int32)[None, :]
        counts = quota[(owner_ids - source_ids) % OWNERS]
        offsets = jnp.cumsum(counts, axis=0) - counts
        slot_perm = jax.vmap(lambda slot_key: jax.random.permutation(slot_key, CPD).astype(jnp.int32))(jax.random.split(key_slots, OWNERS))

        def one_source(source, point_key):
            row_counts = counts[source]
            ends = jnp.cumsum(row_counts)
            positions = jnp.arange(CPD, dtype=jnp.int32)
            owner_seq = jnp.searchsorted(ends, positions, side='right').astype(jnp.int32)
            starts = ends - row_counts
            within = positions - starts[owner_seq]
            slots = slot_perm[owner_seq, offsets[source, owner_seq] + within]
            values = owner_seq * CPD + slots
            shuffle = jax.random.permutation(point_key, CPD).astype(jnp.int32)
            return jnp.zeros((CPD,), jnp.int32).at[shuffle].set(values)
        return jax.vmap(one_source)(jnp.arange(OWNERS, dtype=jnp.int32), jax.random.split(key_points, OWNERS))
    every_group = jax.vmap(one_group)(jax.random.split(key, GROUPS))
    return every_group.reshape(NLAT // 2, NLON // 4).astype(jnp.int32)


def steps_of(stream_key, shape, cuts, smallest, top_value):
    factor_of = 1.0
    for dim, shards_of in cuts:
        heights = jax.random.uniform(jax.random.fold_in(jax.random.fold_in(stream_key, 6), dim), (shards_of,), jnp.float32, smallest / len(cuts), top_value / len(cuts))
        factor_of = factor_of * jnp.repeat(jnp.exp(heights), shape[dim] // shards_of).reshape((-1,) + (1,) * (len(shape) - 1 - dim))
    return factor_of


def normal_values(stream_key, extent, width, reach, shards=(), held_as=jnp.bfloat16):
    drawn = jax.random.normal(stream_key, extent, jnp.float32) * width
    if len(shards) > 0:
        drawn = steps_of(stream_key, extent, shards, -0.22, 0.18) * drawn
    return jnp.clip(drawn, min=-reach, max=reach).astype(held_as)


def setup_inputs(seed: int = 0) -> dict:
    keys = jax.random.split(jax.random.key(seed), 14)
    state = normal_values(keys[0], (LEV, NLAT, NLON), 1.0, 6.0, ((1, 256),))
    dep_row = draw_dep_row(jax.random.fold_in(keys[13], 71), 0)
    dep_col = draw_dep_col(jax.random.fold_in(keys[13], 71), 0)
    row_weight = jnp.clip(1.0 * jax.random.uniform(keys[3], (NLAT, NLON), jnp.float32) ** steps_of(keys[3], (NLAT, NLON), ((0, 256),), -0.2, 0.2), 0.0, 1.0)
    col_weight = jnp.clip(1.0 * jax.random.uniform(keys[4], (NLAT, NLON), jnp.float32) ** steps_of(keys[4], (NLAT, NLON), ((0, 256),), -0.2, 0.2), 0.0, 1.0)
    wave_of = draw_wave_of(jax.random.fold_in(keys[13], 71), 0)
    legendre = draw_legendre(jax.random.fold_in(keys[13], 71), 0)
    gamma = jnp.clip(jnp.exp(jax.random.uniform(keys[7], (LEV,), jnp.float32, math.log(0.3), math.log(30.0))), 0.3, 30.0)
    rad_place = draw_rad_place(jax.random.fold_in(keys[13], 71), 0)
    optics = jnp.clip(jnp.exp(math.log(2.0) - 3.6927934 * jax.random.uniform(keys[9], (DEVS * CPD, LEV), jnp.float32) ** steps_of(keys[9], (DEVS * CPD, LEV), ((0, 256),), -0.2, 0.2)), 0.049804688, 2.0).astype(jnp.bfloat16)
    kabs = jnp.clip(jnp.exp(jax.random.uniform(keys[10], (LEV, GPTS), jnp.float32, math.log(0.02), math.log(0.3))), 0.02, 0.3)
    planck_weight = normal_values(keys[11], (LEV, GPTS), LEV ** -0.5, 1.5, (), jnp.float32)
    kdown = normal_values(keys[12], (GPTS, LEV), GPTS ** -0.5, 0.5, (), jnp.float32)
    return {"state": state, "dep_row": dep_row, "dep_col": dep_col, "row_weight": row_weight, "col_weight": col_weight, "wave_of": wave_of, "legendre": legendre, "gamma": gamma, "rad_place": rad_place, "optics": optics, "kabs": kabs, "planck_weight": planck_weight, "kdown": kdown}


def trig_table(waves):
    lon_index = jnp.arange(NLON, dtype=jnp.int32)[:, None]
    products = lon_index * waves.astype(jnp.int32)[None, :] % NLON
    angles = products.astype(jnp.float32) * (2.0 * math.pi / NLON)
    return jnp.stack([jnp.cos(angles), -jnp.sin(angles)], axis=1).astype(jnp.bfloat16)

def radiate_columns(temps, depths, kabs, planck_weight, kdown):
    emission = 1.0 + jnp.tanh(temps)
    optical = jnp.dot(depths, kabs, precision=lax.Precision.HIGHEST)
    source = jnp.dot(emission, planck_weight, precision=lax.Precision.HIGHEST)
    return jnp.dot(jnp.exp(-optical) * source, kdown, precision=lax.Precision.HIGHEST).astype(jnp.bfloat16)

def reference(state, dep_row, dep_col, row_weight, col_weight, wave_of, legendre, gamma, rad_place, optics, kabs, planck_weight, kdown):
    north_count = NLAT // 2
    scale = math.sqrt(2.0 / NLON)
    upper = dep_row * NLON
    lower = (dep_row + 1) * NLON
    western = dep_col
    eastern = (dep_col + 1) % NLON

    def one_level(layer):
        flat_layer = layer.reshape(-1)

        def fetch(offsets):
            return jnp.take(flat_layer, offsets, axis=0).astype(jnp.float32)
        return ((1.0 - row_weight) * (1.0 - col_weight) * fetch(upper + western) + (1.0 - row_weight) * col_weight * fetch(upper + eastern) + row_weight * (1.0 - col_weight) * fetch(lower + western) + row_weight * col_weight * fetch(lower + eastern)).astype(jnp.bfloat16)
    departed = lax.map(one_level, state)
    harmonics = trig_table(jnp.arange(M, dtype=jnp.int32))
    fourier = (jnp.dot(departed.reshape(LEV * NLAT, NLON), harmonics.reshape(NLON, 2 * M), preferred_element_type=jnp.float32) * scale).astype(jnp.bfloat16)
    fourier = jnp.take(fourier.reshape(LEV, NLAT, 2, M), wave_of, axis=3)
    fourier = jnp.transpose(fourier, (3, 2, 0, 1))
    northern = fourier[..., :north_count].astype(jnp.float32)
    southern = jnp.flip(fourier[..., north_count:], axis=3).astype(jnp.float32)
    symmetric = (northern + southern).astype(jnp.bfloat16)
    antisym = (northern - southern).astype(jnp.bfloat16)
    degree_norm = float(TRUNC * (TRUNC + 1))
    half_steps = jnp.arange(NDEG2, dtype=jnp.int32)

    def one_slot(inputs):
        table_slot, sym_slot, anti_slot, wave = inputs
        legend = table_slot.astype(jnp.float32)
        even_spec = jnp.einsum('hj,qlh->qlj', legend[0], sym_slot.astype(jnp.float32))
        odd_spec = jnp.einsum('hj,qlh->qlj', legend[1], anti_slot.astype(jnp.float32))
        even_deg = (wave + 2 * half_steps).astype(jnp.float32)
        odd_deg = even_deg + 1.0
        even_div = 1.0 + gamma[:, None] * (even_deg * (even_deg + 1.0))[None, :] / degree_norm
        odd_div = 1.0 + gamma[:, None] * (odd_deg * (odd_deg + 1.0))[None, :] / degree_norm
        even_sol = (even_spec / even_div[None]).astype(jnp.bfloat16)
        odd_sol = (odd_spec / odd_div[None]).astype(jnp.bfloat16)
        even_grid = 4.0 * jnp.einsum('hj,qlj->qlh', legend[0], even_sol.astype(jnp.float32))
        odd_grid = 4.0 * jnp.einsum('hj,qlj->qlh', legend[1], odd_sol.astype(jnp.float32))
        return ((even_grid + odd_grid).astype(jnp.bfloat16), (even_grid - odd_grid).astype(jnp.bfloat16))
    north_out, south_out = lax.map(one_slot, (legendre, symmetric, antisym, wave_of))
    grid_four = jnp.concatenate([north_out, jnp.flip(south_out, axis=3)], axis=3)
    grid_four = jnp.transpose(grid_four, (1, 0, 2, 3)).reshape(2 * M, LEV * NLAT)
    slot_table = jnp.take(harmonics, wave_of, axis=2).reshape(NLON, 2 * M)
    dynamics = jnp.dot(slot_table, grid_four, preferred_element_type=jnp.float32) * scale
    dynamics = jnp.transpose(dynamics.reshape(NLON, LEV, NLAT), (1, 2, 0))
    blocks = state.astype(jnp.float32).reshape(LEV, NLAT // 2, 2, NLON // 4, 4)
    coarse_temp = (lax.optimization_barrier(jnp.sum(blocks, axis=(2, 4))) * 0.125).astype(jnp.bfloat16)
    temps = jnp.transpose(coarse_temp, (1, 2, 0)).reshape(-1, LEV).astype(jnp.float32)
    group_rows = OWNERS * (ROWS_DEV // 2)
    group_of = jnp.arange(NLAT // 2, dtype=jnp.int32) // group_rows
    optic_index = (group_of[:, None] * (OWNERS * CPD) + rad_place).reshape(-1)
    depths = jnp.take(optics, optic_index, axis=0).astype(jnp.float32)
    heating = radiate_columns(temps, depths, kabs, planck_weight, kdown)
    heating = jnp.transpose(heating.reshape(NLAT // 2, NLON // 4, LEV), (2, 0, 1))
    heating = jnp.broadcast_to(heating[:, :, None, :, None], (LEV, NLAT // 2, 2, NLON // 4, 4)).reshape(LEV, NLAT, NLON)
    return (dynamics + heating.astype(jnp.float32)).astype(jnp.bfloat16)
```

```python
import functools
import math

import jax
import jax.numpy as jnp
from jax import lax
from jax.experimental import pallas as pl
from jax.experimental.pallas import tpu as pltpu
from jax.sharding import PartitionSpec as P

F32 = jnp.float32
BF16 = jnp.bfloat16
RADIX = 32
HALF = RADIX // 2 + 1
VMEM_LIMIT = 48 * 1024 * 1024
MESH = pl.DeviceIdType.MESH


def cplx(angle_num, angle_den):
    turn = 2.0 * math.pi * angle_num / angle_den
    return math.cos(turn), math.sin(turn)


def real_fft(planes):
    count = len(planes)
    if count == 2:
        return [(planes[0] + planes[1], None), (planes[0] - planes[1], None)]
    even = real_fft(planes[0::2])
    odd = real_fft(planes[1::2])
    half = count // 2
    out = []
    for k in range(half + 1):

        def pick(spec):
            kk = k % half
            if kk <= half // 2:
                return spec[kk]
            re, im = spec[half - kk]
            return re, (None if im is None else -im)

        er, ei = pick(even)
        orr, oi = pick(odd)
        c, s = cplx(k, count)
        if k == 0:
            out.append((er + orr, None))
        elif k == half:
            out.append((er - orr, None))
        elif 4 * k == count:
            out.append((er, -orr))
        else:
            if oi is None:
                tr, ti = c * orr, -s * orr
            else:
                tr, ti = c * orr + s * oi, c * oi - s * orr
            out.append((er + tr, ti if ei is None else ei + ti))
    return out


def real_ifft(spec):
    half = len(spec) - 1
    count = 2 * half
    if count == 2:
        return [spec[0][0] + spec[1][0], spec[0][0] - spec[1][0]]
    even, odd = [], []
    for k in range(half // 2 + 1):
        xr, xi = spec[k]
        yr, yi = spec[half - k]
        if k == 0:
            even.append((xr + yr, None))
            odd.append((xr - yr, None))
        elif 2 * k == half:
            even.append((xr + xr, None))
            odd.append((-(xi + xi), None))
        else:
            even.append((xr + yr, xi - yi))
            dr, di = xr - yr, xi + yi
            c, s = cplx(k, count)
            odd.append((c * dr - s * di, c * di + s * dr))
    ev, od = real_ifft(even), real_ifft(odd)
    return [plane for pair in zip(ev, od) for plane in pair]


def forward_kernel(
    row_start_ref, prev_ref, own_ref, next_ref, row_ref, col_ref, rw_ref, cw_ref,
    table_ref, fold_ref, out_ref, rows_ref, departed_ref, z_ref, ft_ref,
):
    lon = own_ref.shape[2]
    levels = own_ref.shape[1]
    for i in range(2):
        rows_ref[i] = prev_ref[i].astype(F32)
        rows_ref[2 + i] = own_ref[i].astype(F32)
        rows_ref[4 + i] = next_ref[i].astype(F32)
    sub = lax.broadcasted_iota(jnp.int32, (8, lon), 0) - 2
    lon_ids = lax.broadcasted_iota(jnp.int32, (1, lon), 1)
    start = row_start_ref[0]
    for i in range(2):
        rel_row = row_ref[i : i + 1, :] - (start + i)
        rel_col = (col_ref[i : i + 1, :] - lon_ids + 2) & (lon - 1)
        rel_col = rel_col - 2
        a = rw_ref[i : i + 1, :]
        b = cw_ref[i : i + 1, :]
        row_w = jnp.where(rel_row == sub, 1.0 - a, 0.0) + jnp.where(rel_row == sub - 1, a, 0.0)
        col_w = jnp.where(rel_col == sub, 1.0 - b, 0.0) + jnp.where(rel_col == sub - 1, b, 0.0)
        shifted = [
            row_w if dc == 0 else pltpu.roll(row_w, dc % lon, 1) for dc in range(-2, 4)
        ]
        for h in range(levels // 8):
            total = None
            for dc in range(-2, 4):
                mixed = None
                for dr in range(5):
                    term = shifted[dc + 2][dr : dr + 1, :] * rows_ref[i + dr, 8 * h : 8 * h + 8, :]
                    mixed = term if mixed is None else mixed + term
                if dc != 0:
                    mixed = pltpu.roll(mixed, (-dc) % lon, 1)
                term = col_w[dc + 2 : dc + 3, :] * mixed
                total = term if total is None else total + term
            departed_ref[i, 8 * h : 8 * h + 8, :] = total
    for i in range(2):
        planes = [
            departed_ref[i, :, 128 * j : 128 * j + 128].astype(BF16).astype(F32)
            for j in range(RADIX)
        ]
        for k, (re, im) in enumerate(real_fft(planes)):
            at = 2 * levels * k + levels * i
            z_ref[at : at + levels, 0:128] = re.astype(BF16)
            z_ref[at : at + levels, 128:256] = (
                jnp.zeros((levels, 128), BF16) if im is None else im.astype(BF16)
            )
    scale = math.sqrt(2.0 / lon)
    r = 2 * levels
    for c in range(8):
        prod = lax.dot_general(
            z_ref[...], table_ref[256 * c : 256 * c + 256, :],
            (((1,), (1,)), ((), ())), preferred_element_type=F32,
        )
        fold = fold_ref[c // 2 : c // 2 + 1, :]
        got = prod[0:r]
        for k in range(1, HALF):
            got = jnp.where(fold == k, prod[r * k : r * k + r], got)
        got = got * scale
        for i in range(2):
            ft_ref[128 * i + 16 * c : 128 * i + 16 * c + 16, :] = got[16 * i : 16 * i + 16]
    swapped = jnp.transpose(ft_ref[...])
    parts = [swapped[:, 128 * i : 128 * i + 128].reshape(32, 1, 8, 128) for i in range(2)]
    out_ref[...] = jnp.concatenate(parts, axis=1).reshape(512, 128).astype(BF16)


def inverse_kernel(got_ref, table_ref, fold_ref, heat_ref, out_ref, e_ref):
    levels = heat_ref.shape[0]
    lon = out_ref.shape[2]
    r = 2 * levels
    rows = got_ref[...].astype(F32).reshape(32, 2, 8, 128)
    turned = [jnp.transpose(rows[:, i].reshape(256, 128)) for i in range(2)]
    for c in range(8):
        piece = jnp.concatenate([t[16 * c : 16 * c + 16] for t in turned], axis=0)
        fold = fold_ref[c // 2 : c // 2 + 1, :]
        for k in range(HALF):
            e_ref[r * k : r * k + r, 256 * c : 256 * c + 256] = jnp.where(
                fold == k, piece, 0.0
            ).astype(BF16)
    waves = jnp.dot(e_ref[...], table_ref[...], preferred_element_type=F32)
    low = lax.broadcasted_iota(jnp.int32, (128, 512), 0)
    high = lax.broadcasted_iota(jnp.int32, (128, 512), 1)
    spread = jnp.where(low == high // 4, 1.0, 0.0).astype(BF16)
    heat = [
        jnp.dot(heat_ref[:, 128 * b : 128 * b + 128], spread, preferred_element_type=F32)
        for b in range(lon // 512)
    ]
    scale = 0.5 * math.sqrt(2.0 / lon)
    for i in range(2):
        spec = []
        for k in range(HALF):
            at = r * k + levels * i
            block = waves[at : at + levels]
            re, im = block[:, 0:128], block[:, 128:256]
            if k in (0, HALF - 1):
                spec.append((re + re, None))
            else:
                spec.append((re, im))
        for j, plane in enumerate(real_ifft(spec)):
            warm = heat[j // 4][:, 128 * (j % 4) : 128 * (j % 4) + 128]
            out_ref[i, :, 128 * j : 128 * j + 128] = (plane * scale + warm).astype(BF16)


def radiation_kernel(own_ref, place_ref, optics_ref, kabs_ref, planck_ref, kdown_ref, out_ref):
    levels = own_ref.shape[1]
    lon = own_ref.shape[2]
    cols = lon // 4
    high = lax.broadcasted_iota(jnp.int32, (512, 128), 0)
    low = lax.broadcasted_iota(jnp.int32, (512, 128), 1)
    pool = jnp.where(high // 4 == low, 1.0, 0.0).astype(BF16)
    temps = []
    for b in range(lon // 512):
        part = None
        for e in range(2):
            term = jnp.dot(
                own_ref[e, :, 512 * b : 512 * b + 512], pool, preferred_element_type=F32
            )
            part = term if part is None else part + term
        temps.append(part)
    temps = (jnp.concatenate(temps, axis=1) * 0.125).astype(BF16).astype(F32)
    place = place_ref[...]
    slot = place & (cols - 1)
    owner = place // cols
    depth_all = None
    for b in range(cols // 256):
        ids = lax.broadcasted_iota(jnp.int32, (256, cols), 0) + 256 * b
        hot = jnp.where(ids == slot, 1.0, 0.0).astype(BF16)
        term = jnp.dot(
            optics_ref[:, 256 * b : 256 * b + 256], hot, preferred_element_type=F32
        )
        depth_all = term if depth_all is None else depth_all + term
    depth = depth_all[0:levels]
    for o in range(1, optics_ref.shape[0] // levels):
        depth = jnp.where(owner == o, depth_all[levels * o : levels * o + levels], depth)
    best = lax.Precision.HIGHEST
    emission = 1.0 + jnp.tanh(temps)
    optical = jnp.dot(kabs_ref[...], depth, precision=best, preferred_element_type=F32)
    source = jnp.dot(planck_ref[...], emission, precision=best, preferred_element_type=F32)
    out_ref[...] = jnp.dot(
        kdown_ref[...], jnp.exp(-optical) * source, precision=best, preferred_element_type=F32
    ).astype(BF16)


def one_hot(shape, want):
    rows = lax.broadcasted_iota(jnp.int32, shape, 0)
    cols = lax.broadcasted_iota(jnp.int32, shape, 1)
    return jnp.where(want(rows) == cols, 1.0, 0.0).astype(BF16)


def lat_first(row):
    return (row % 32) * 16 + ((row // 32) % 2) * 8 + row // 64


def group_first(row):
    return (row % 8) * 64 + ((row // 8) % 2) * 32 + row // 16


def natural(row):
    return (row // 64) * 64 + (row % 2) * 32 + (row % 64) // 2


def unnatural(row):
    return (row // 64) * 64 + (row % 32) * 2 + (row % 64) // 32


def permuted(matrix, data):
    return jnp.dot(matrix, data, preferred_element_type=F32)


def legendre_step(north_in, south_in, table_ref, gamma_ref, waves_ref, turn, trunc):
    to_north, to_south, from_north, from_south = turn
    north = permuted(to_north, north_in)
    south = permuted(to_south, south_in)
    sym = jnp.transpose(north + south).astype(BF16)
    anti = jnp.transpose(north - south).astype(BF16)
    half_degree = table_ref.shape[3]
    steps = lax.broadcasted_iota(jnp.int32, (1, half_degree), 1)
    norm = float(trunc * (trunc + 1))
    gamma = gamma_ref[...]
    even_rows, odd_rows = [], []
    for s in range(4):
        pair = []
        for p, source in enumerate((sym, anti)):
            table = table_ref[s, p]
            spec = jnp.dot(source[32 * s : 32 * s + 32], table, preferred_element_type=F32)
            degree = (waves_ref[s] + 2 * steps + p).astype(F32)
            divisor = 1.0 + gamma * (degree * (degree + 1.0)) / norm
            solved = (spec / divisor).astype(BF16)
            pair.append(
                4.0
                * lax.dot_general(
                    solved, table, (((1,), (1,)), ((), ())), preferred_element_type=F32
                )
            )
        even_rows.append(pair[0])
        odd_rows.append(pair[1])
    even = jnp.concatenate(even_rows, axis=0)
    odd = jnp.concatenate(odd_rows, axis=0)
    north = jnp.transpose(even + odd).astype(BF16)
    south = jnp.transpose(even - odd).astype(BF16)
    return permuted(from_north, north).astype(BF16), permuted(from_south, south).astype(BF16)


def middle_kernel(
    trunc, sent_ref, table_ref, gamma_ref, waves_ref, out_ref,
    got1, send2, got2, send3, got3, send4,
    send_lat, recv_lat, send_grp, recv_grp, send_grp2, recv_grp2, send_lat2, recv_lat2,
):
    g = lax.axis_index("grp")
    a = lax.axis_index("lat")
    barrier = pltpu.get_barrier_semaphore()

    @pl.loop(1, 32)
    def _(k):
        pl.semaphore_signal(
            barrier, inc=1, device_id=(g, lax.rem(a + k, 32)), device_id_type=MESH
        )

    @pl.loop(1, 8)
    def _(k):
        pl.semaphore_signal(
            barrier, inc=1, device_id=(lax.rem(g + k, 8), a), device_id_type=MESH
        )

    pl.semaphore_wait(barrier, 38)

    def exchange(source, target, block, send_sems, recv_sems, count, mine, peer_of):
        def copy(k):
            peer = lax.rem(mine + k, count)
            return pltpu.make_async_remote_copy(
                src_ref=source.at[pl.ds(pl.multiple_of(peer * block, block), block)],
                dst_ref=target.at[pl.ds(pl.multiple_of(mine * block, block), block)],
                send_sem=send_sems.at[k],
                recv_sem=recv_sems.at[k],
                device_id=peer_of(peer),
                device_id_type=MESH,
            )

        def arrival(k):
            peer = lax.rem(mine + count - k, count)
            return pltpu.make_async_remote_copy(
                src_ref=source.at[pl.ds(pl.multiple_of(peer * block, block), block)],
                dst_ref=target.at[pl.ds(pl.multiple_of(peer * block, block), block)],
                send_sem=send_sems.at[k],
                recv_sem=recv_sems.at[k],
                device_id=peer_of(peer),
                device_id_type=MESH,
            )

        @pl.loop(1, count)
        def _(k):
            copy(k).start()

        here = pl.ds(pl.multiple_of(mine * block, block), block)
        target[here, :] = source[here, :]

        def finish():
            @pl.loop(1, count)
            def _(k):
                copy(k).wait_send()
                arrival(k).wait_recv()

        return finish

    def over_lat(peer):
        return (g, peer)

    def over_grp(peer):
        return (peer, a)

    done = exchange(sent_ref, got1, 16, send_lat, recv_lat, 32, a, over_lat)
    to_group = one_hot((512, 512), lat_first)
    done()
    send2[...] = permuted(to_group, got1[...]).astype(BF16)
    done = exchange(send2, got2, 64, send_grp, recv_grp, 8, g, over_grp)
    turn = (
        one_hot((256, 256), natural),
        one_hot((256, 256), lambda row: natural(255 - row)),
        one_hot((256, 256), unnatural),
        one_hot((256, 256), lambda row: 255 - unnatural(row)),
    )
    done()
    north, south = legendre_step(
        got2[0:256, :], got2[256:512, :], table_ref, gamma_ref, waves_ref, turn, trunc
    )
    send3[0:256, :] = north
    send3[256:512, :] = south
    done = exchange(send3, got3, 64, send_grp2, recv_grp2, 8, g, over_grp)
    to_lat = one_hot((512, 512), group_first)
    done()
    send4[...] = permuted(to_lat, got3[...]).astype(BF16)
    exchange(send4, out_ref, 16, send_lat2, recv_lat2, 32, a, over_lat)()


def vmem(count):
    return [pl.BlockSpec(memory_space=pltpu.VMEM)] * count


def shards(
    state, dep_row, dep_col, row_weight, col_weight, wave_of, legendre, gamma,
    rad_place, optics, kabs, planck_weight, kdown,
):
    levels, lat_rows, lon = state.shape
    groups = lax.axis_size("grp")
    owners = lax.axis_size("lat")
    total_waves = wave_of.shape[0]
    dev_index = lax.axis_index("grp") * owners + lax.axis_index("lat")
    params = pltpu.CompilerParams(vmem_limit_bytes=VMEM_LIMIT)

    own = jnp.transpose(state, (1, 0, 2))
    devices = groups * owners
    up = [(i, i + 1) for i in range(devices - 1)]
    down = [(i + 1, i) for i in range(devices - 1)]
    before = lax.ppermute(own, ("grp", "lat"), up)
    after = lax.ppermute(own, ("grp", "lat"), down)
    optics_all = lax.all_gather(jnp.transpose(optics), "lat", axis=0, tiled=True)

    waves = wave_of.reshape(groups, owners, 4).transpose(2, 1, 0).reshape(4, devices)
    class_of = waves % RADIX
    fold = jnp.minimum(class_of, RADIX - class_of)
    points = waves[:, :, None] * jnp.arange(128, dtype=jnp.int32)[None, None, :] % lon
    angles = points.astype(F32) * (2.0 * math.pi / lon)
    cosine, sine = jnp.cos(angles), jnp.sin(angles)
    side = jnp.where(class_of > RADIX // 2, -1.0, 1.0)[:, :, None]
    table = jnp.stack(
        [
            jnp.concatenate([cosine, side * sine], axis=2),
            jnp.concatenate([-sine, side * cosine], axis=2),
        ],
        axis=1,
    ).astype(BF16).reshape(8 * devices, 256)

    outbound = pl.pallas_call(
        forward_kernel,
        out_shape=jax.ShapeDtypeStruct((2 * devices, 128), BF16),
        in_specs=[pl.BlockSpec(memory_space=pltpu.SMEM)] + vmem(9),
        out_specs=pl.BlockSpec(memory_space=pltpu.VMEM),
        scratch_shapes=[
            pltpu.VMEM((6, levels, lon), F32),
            pltpu.VMEM((2, levels, lon), F32),
            pltpu.VMEM((HALF * 2 * levels, 256), BF16),
            pltpu.VMEM((256, 256), F32),
        ],
        compiler_params=params,
        name="interp_fourier",
    )(
        (dev_index * lat_rows).astype(jnp.int32).reshape(1), before, own, after,
        dep_row, dep_col, row_weight, col_weight, table, fold,
    )

    heat = pl.pallas_call(
        radiation_kernel,
        out_shape=jax.ShapeDtypeStruct((levels, lon // 4), BF16),
        in_specs=vmem(6),
        out_specs=pl.BlockSpec(memory_space=pltpu.VMEM),
        compiler_params=params,
        name="radiation",
    )(own, rad_place, optics_all, kabs.T, planck_weight.T, kdown.T)

    my_waves = lax.dynamic_slice_in_dim(wave_of, dev_index * 4, 4)
    rows = 2 * devices
    inbound = pl.pallas_call(
        functools.partial(middle_kernel, total_waves - 1),
        out_shape=jax.ShapeDtypeStruct((rows, 128), BF16),
        in_specs=vmem(3) + [pl.BlockSpec(memory_space=pltpu.SMEM)],
        out_specs=pl.BlockSpec(memory_space=pltpu.VMEM),
        scratch_shapes=[pltpu.VMEM((rows, 128), BF16)] * 6
        + [
            pltpu.SemaphoreType.DMA((32,)),
            pltpu.SemaphoreType.DMA((32,)),
            pltpu.SemaphoreType.DMA((8,)),
            pltpu.SemaphoreType.DMA((8,)),
            pltpu.SemaphoreType.DMA((8,)),
            pltpu.SemaphoreType.DMA((8,)),
            pltpu.SemaphoreType.DMA((32,)),
            pltpu.SemaphoreType.DMA((32,)),
        ],
        compiler_params=pltpu.CompilerParams(
            vmem_limit_bytes=VMEM_LIMIT, collective_id=0, has_side_effects=True
        ),
        name="legendre_exchange",
    )(outbound, legendre, jnp.tile(gamma, 2)[:, None], my_waves)

    result = pl.pallas_call(
        inverse_kernel,
        out_shape=jax.ShapeDtypeStruct((lat_rows, levels, lon), BF16),
        in_specs=vmem(4),
        out_specs=pl.BlockSpec(memory_space=pltpu.VMEM),
        scratch_shapes=[pltpu.VMEM((HALF * 2 * levels, 8 * devices), BF16)],
        compiler_params=params,
        name="inverse_fourier",
    )(inbound, table, fold, heat)
    return jnp.transpose(result, (1, 0, 2))


def solution(mesh):
    return jax.shard_map(
        shards,
        mesh=mesh,
        in_specs=(
            P(None, ("grp", "lat"), None),
            P(("grp", "lat"), None),
            P(("grp", "lat"), None),
            P(("grp", "lat"), None),
            P(("grp", "lat"), None),
            P(),
            P(("grp", "lat"), None, None, None),
            P(),
            P(("grp", "lat"), None),
            P(("grp", "lat"), None),
            P(),
            P(),
            P(),
        ),
        out_specs=P(None, ("grp", "lat"), None),
        check_vma=False,
    )
```

```python
import functools
import math

import jax
import jax.numpy as jnp
from jax import lax
from jax.experimental import pallas as pl
from jax.experimental.pallas import tpu as pltpu
from jax.sharding import PartitionSpec as P

F32 = jnp.float32
BF16 = jnp.bfloat16
RADIX = 32
HALF = RADIX // 2 + 1
VMEM_LIMIT = 62 * 1024 * 1024
MESH = pl.DeviceIdType.MESH


def cplx(angle_num, angle_den):
    turn = 2.0 * math.pi * angle_num / angle_den
    return math.cos(turn), math.sin(turn)


def real_fft(planes):
    count = len(planes)
    if count == 2:
        return [(planes[0] + planes[1], None), (planes[0] - planes[1], None)]
    even = real_fft(planes[0::2])
    odd = real_fft(planes[1::2])
    half = count // 2
    out = []
    for k in range(half + 1):

        def pick(spec):
            kk = k % half
            if kk <= half // 2:
                return spec[kk]
            re, im = spec[half - kk]
            return re, (None if im is None else -im)

        er, ei = pick(even)
        orr, oi = pick(odd)
        c, s = cplx(k, count)
        if k == 0:
            out.append((er + orr, None))
        elif k == half:
            out.append((er - orr, None))
        elif 4 * k == count:
            out.append((er, -orr))
        else:
            if oi is None:
                tr, ti = c * orr, -s * orr
            else:
                tr, ti = c * orr + s * oi, c * oi - s * orr
            out.append((er + tr, ti if ei is None else ei + ti))
    return out


def real_ifft(spec):
    half = len(spec) - 1
    count = 2 * half
    if count == 2:
        return [spec[0][0] + spec[1][0], spec[0][0] - spec[1][0]]
    even, odd = [], []
    for k in range(half // 2 + 1):
        xr, xi = spec[k]
        yr, yi = spec[half - k]
        if k == 0:
            even.append((xr + yr, None))
            odd.append((xr - yr, None))
        elif 2 * k == half:
            even.append((xr + xr, None))
            odd.append((-(xi + xi), None))
        else:
            even.append((xr + yr, xi - yi))
            dr, di = xr - yr, xi + yi
            c, s = cplx(k, count)
            odd.append((c * dr - s * di, c * di + s * dr))
    ev, od = real_ifft(even), real_ifft(odd)
    return [plane for pair in zip(ev, od) for plane in pair]


def one_hot(shape, want):
    rows = lax.broadcasted_iota(jnp.int32, shape, 0)
    cols = lax.broadcasted_iota(jnp.int32, shape, 1)
    return jnp.where(want(rows) == cols, 1.0, 0.0).astype(BF16)


def lat_first(row):
    return (row % 32) * 16 + ((row // 32) % 2) * 8 + row // 64


def group_first(row):
    return (row % 8) * 64 + ((row // 8) % 2) * 32 + row // 16


def natural(row):
    return (row // 64) * 64 + (row % 2) * 32 + (row % 64) // 2


def unnatural(row):
    return (row // 64) * 64 + (row % 32) * 2 + (row % 64) // 32


def permuted(matrix, data):
    return jnp.dot(matrix, data, preferred_element_type=F32)


def legendre_step(north_in, south_in, table_ref, gamma, waves_ref, first, turn, trunc):
    to_north, to_south, from_north, from_south = turn
    north = permuted(to_north, north_in)
    south = permuted(to_south, south_in)
    sym = jnp.transpose(north + south).astype(BF16)
    anti = jnp.transpose(north - south).astype(BF16)
    half_degree = table_ref.shape[3]
    steps = lax.broadcasted_iota(jnp.int32, (1, half_degree), 1)
    norm = float(trunc * (trunc + 1))
    even_rows, odd_rows = [], []
    for s in range(4):
        pair = []
        for p, source in enumerate((sym, anti)):
            table = table_ref[s, p]
            spec = jnp.dot(source[32 * s : 32 * s + 32], table, preferred_element_type=F32)
            degree = (waves_ref[first + s] + 2 * steps + p).astype(F32)
            divisor = 1.0 + gamma * (degree * (degree + 1.0)) / norm
            solved = (spec / divisor).astype(BF16)
            pair.append(
                4.0
                * lax.dot_general(
                    solved, table, (((1,), (1,)), ((), ())), preferred_element_type=F32
                )
            )
        even_rows.append(pair[0])
        odd_rows.append(pair[1])
    even = jnp.concatenate(even_rows, axis=0)
    odd = jnp.concatenate(odd_rows, axis=0)
    north = jnp.transpose(even + odd).astype(BF16)
    south = jnp.transpose(even - odd).astype(BF16)
    return permuted(from_north, north).astype(BF16), permuted(from_south, south).astype(BF16)


def interpolate(start, sources, row_ref, col_ref, rw_ref, cw_ref, departed_ref):
    levels, lon = departed_ref.shape[1:]
    sub = lax.broadcasted_iota(jnp.int32, (8, lon), 0) - 2
    lon_ids = lax.broadcasted_iota(jnp.int32, (1, lon), 1)
    for i in range(2):
        rel_row = row_ref[i : i + 1, :] - (start + i)
        rel_col = ((col_ref[i : i + 1, :] - lon_ids + 2) & (lon - 1)) - 2
        a = rw_ref[i : i + 1, :]
        b = cw_ref[i : i + 1, :]
        row_w = jnp.where(rel_row == sub, 1.0 - a, 0.0) + jnp.where(rel_row == sub - 1, a, 0.0)
        col_w = jnp.where(rel_col == sub, 1.0 - b, 0.0) + jnp.where(rel_col == sub - 1, b, 0.0)
        shifted = [
            row_w if dc == 0 else pltpu.roll(row_w, dc % lon, 1) for dc in range(-2, 4)
        ]
        for h in range(levels // 8):
            total = None
            for dc in range(-2, 4):
                mixed = None
                for dr in range(5):
                    term = shifted[dc + 2][dr : dr + 1, :] * sources[i + dr, 8 * h : 8 * h + 8, :]
                    mixed = term if mixed is None else mixed + term
                if dc != 0:
                    mixed = pltpu.roll(mixed, (-dc) % lon, 1)
                term = col_w[dc + 2 : dc + 3, :] * mixed
                total = term if total is None else total + term
            departed_ref[i, 8 * h : 8 * h + 8, :] = total


def forward_waves(departed_ref, z_ref, table_ref, fold, ft_ref, out_ref):
    levels, lon = departed_ref.shape[1:]
    for i in range(2):
        planes = [
            departed_ref[i, :, 128 * j : 128 * j + 128].astype(BF16).astype(F32)
            for j in range(RADIX)
        ]
        for k, (re, im) in enumerate(real_fft(planes)):
            at = 2 * levels * k + levels * i
            z_ref[at : at + levels, 0:128] = re.astype(BF16)
            z_ref[at : at + levels, 128:256] = (
                jnp.zeros((levels, 128), BF16) if im is None else im.astype(BF16)
            )
    scale = math.sqrt(2.0 / lon)
    r = 2 * levels
    for c in range(8):
        prod = lax.dot_general(
            z_ref[...], table_ref[256 * c : 256 * c + 256, :],
            (((1,), (1,)), ((), ())), preferred_element_type=F32,
        )
        got = prod[0:r]
        for k in range(1, HALF):
            got = jnp.where(fold[c // 2] == k, prod[r * k : r * k + r], got)
        got = got * scale
        for i in range(2):
            ft_ref[128 * i + 16 * c : 128 * i + 16 * c + 16, :] = got[16 * i : 16 * i + 16]
    swapped = jnp.transpose(ft_ref[...])
    parts = [swapped[:, 128 * i : 128 * i + 128].reshape(32, 1, 8, 128) for i in range(2)]
    out_ref[...] = jnp.concatenate(parts, axis=1).reshape(512, 128).astype(BF16)


def inverse_waves(got_ref, table_ref, fold, heat, e_ref, out_ref):
    levels, lon = out_ref.shape[1:]
    r = 2 * levels
    rows = got_ref[...].astype(F32).reshape(32, 2, 8, 128)
    turned = [jnp.transpose(rows[:, i].reshape(256, 128)) for i in range(2)]
    for c in range(8):
        piece = jnp.concatenate([t[16 * c : 16 * c + 16] for t in turned], axis=0)
        for k in range(HALF):
            e_ref[r * k : r * k + r, 256 * c : 256 * c + 256] = jnp.where(
                fold[c // 2] == k, piece, 0.0
            ).astype(BF16)
    waves = jnp.dot(e_ref[...], table_ref[...], preferred_element_type=F32)
    scale = 0.5 * math.sqrt(2.0 / lon)
    for i in range(2):
        spec = []
        for k in range(HALF):
            at = r * k + levels * i
            block = waves[at : at + levels]
            re, im = block[:, 0:128], block[:, 128:256]
            if k in (0, HALF - 1):
                spec.append((re + re, None))
            else:
                spec.append((re, im))
        for j, plane in enumerate(real_ifft(spec)):
            warm = heat[:, 128 * j : 128 * j + 128]
            out_ref[i, :, 128 * j : 128 * j + 128] = (plane * scale + warm).astype(BF16)


def coarse_means(own_ref):
    lon = own_ref.shape[2]
    high = lax.broadcasted_iota(jnp.int32, (512, 128), 0)
    low = lax.broadcasted_iota(jnp.int32, (512, 128), 1)
    pool = jnp.where(high // 4 == low, 1.0, 0.0).astype(BF16)
    temps = []
    for b in range(lon // 512):
        part = None
        for e in range(2):
            term = jnp.dot(
                own_ref[e, :, 512 * b : 512 * b + 512], pool, preferred_element_type=F32
            )
            part = term if part is None else part + term
        temps.append(part)
    return (jnp.concatenate(temps, axis=1) * 0.125).astype(BF16).astype(F32)


def radiate(temps, place, optics_ref, kabs, planck, kdown):
    levels, cols = temps.shape
    slot = place & (cols - 1)
    owner = place // cols
    block = (owner & 1) * 16 + owner // 2
    depth_all = None
    for b in range(cols // 256):
        ids = lax.broadcasted_iota(jnp.int32, (256, cols), 0) + 256 * b
        hot = jnp.where(ids == slot, 1.0, 0.0).astype(BF16)
        term = jnp.dot(
            optics_ref[:, 256 * b : 256 * b + 256], hot, preferred_element_type=F32
        )
        depth_all = term if depth_all is None else depth_all + term
    depth = depth_all[0:levels]
    for o in range(1, optics_ref.shape[0] // levels):
        depth = jnp.where(block == o, depth_all[levels * o : levels * o + levels], depth)
    best = lax.Precision.HIGHEST
    emission = 1.0 + jnp.tanh(temps)
    optical = jnp.dot(kabs, depth, precision=best, preferred_element_type=F32)
    source = jnp.dot(planck, emission, precision=best, preferred_element_type=F32)
    return jnp.dot(
        kdown, jnp.exp(-optical) * source, precision=best, preferred_element_type=F32
    ).astype(BF16)


def spread_heat(heat, lon):
    low = lax.broadcasted_iota(jnp.int32, (128, 512), 0)
    high = lax.broadcasted_iota(jnp.int32, (128, 512), 1)
    spread = jnp.where(low == high // 4, 1.0, 0.0).astype(BF16)
    return jnp.concatenate(
        [
            jnp.dot(heat[:, 128 * b : 128 * b + 128], spread, preferred_element_type=F32)
            for b in range(lon // 512)
        ],
        axis=1,
    )


def slot_waves(wave_tile):
    lane = lax.broadcasted_iota(jnp.int32, (128, 1024), 0)
    spot = lax.broadcasted_iota(jnp.int32, (128, 1024), 1)
    pick = jnp.where(lane == 4 * ((spot & 255) // 8) + spot // 256, 1.0, 0.0).astype(BF16)
    high = (wave_tile // 32).astype(F32).astype(BF16)
    low = (wave_tile & 31).astype(F32).astype(BF16)
    spread = 32.0 * jnp.dot(high, pick, preferred_element_type=F32) + jnp.dot(
        low, pick, preferred_element_type=F32
    )
    group = lax.broadcasted_iota(jnp.int32, (8, 1024), 0)
    spot = lax.broadcasted_iota(jnp.int32, (8, 1024), 1)
    flat = jnp.sum(jnp.where(group == (spot & 7), spread, 0.0), axis=0, keepdims=True)
    return [flat[:, 256 * s : 256 * s + 256] for s in range(4)]


def wave_table(rows, table_ref, lon):
    fold = []
    for row in rows:
        kind = row.astype(jnp.int32) & (RADIX - 1)
        fold.append(jnp.minimum(kind, RADIX - kind))
    stacked = jnp.concatenate(rows + [jnp.zeros((124, 256), F32)], axis=0)
    columns = jnp.transpose(stacked)
    step = lax.broadcasted_iota(jnp.int32, (256, 128), 1)
    quarter = lon // 4
    for s in range(4):
        wave = columns[:, s : s + 1].astype(jnp.int32)
        point = (wave * step) & (lon - 1)
        turn = (point + quarter // 2) // quarter
        x = (point - turn * quarter).astype(F32) * (2.0 * math.pi / lon)
        y = x * x
        cosine = 1.0 + y * (-0.5 + y * (1.0 / 24 + y * (-1.0 / 720 + y * (1.0 / 40320))))
        sine = x * (1.0 + y * (-1.0 / 6 + y * (1.0 / 120 + y * (-1.0 / 5040 + y / 362880))))
        swap = (turn & 1) == 1
        c = jnp.where(swap, sine, cosine)
        n = jnp.where(swap, cosine, sine)
        c = jnp.where(((turn + 1) & 2) == 2, -c, c)
        n = jnp.where((turn & 2) == 2, -n, n)
        side = jnp.where((wave & (RADIX - 1)) > RADIX // 2, -1.0, 1.0)
        at = 512 * s
        table_ref[at : at + 256, 0:128] = c.astype(BF16)
        table_ref[at : at + 256, 128:256] = (side * n).astype(BF16)
        table_ref[at + 256 : at + 512, 0:128] = (-n).astype(BF16)
        table_ref[at + 256 : at + 512, 128:256] = (side * c).astype(BF16)
    return fold


def level_column(gamma_ref, rows):
    at = lax.broadcasted_iota(jnp.int32, (rows, 1), 0)
    levels = gamma_ref.shape[0]
    column = jnp.zeros((rows, 1), F32)
    for l in range(levels):
        column = jnp.where(at % levels == l, gamma_ref[l], column)
    return column


def tall(matrix):
    return jnp.transpose(jnp.concatenate([matrix, jnp.zeros((112, 128), F32)], axis=0))[:, 0:16]


def step_kernel(
    trunc, own_ref, row_hbm, col_hbm, rw_hbm, cw_hbm, waves_ref, wave_tile_ref, legendre_hbm,
    gamma_ref, place_hbm, optics_ref, kabs_ref, planck_ref, kdown_ref, out_ref,
    row_ref, col_ref, rw_ref, cw_ref, legendre_ref, place_ref,
    before, after, sources, departed, table, z_ref, ft_ref, e_ref, optics_all,
    sent, got1, send2, got2, send3, got3, send4, got4,
    load_sems, halo_send, halo_recv, opt_send, opt_recv, relay_send, relay_recv,
    send_lat, recv_lat, send_grp, recv_grp, send_grp2, recv_grp2, send_lat2, recv_lat2,
):
    g = lax.axis_index("grp")
    a = lax.axis_index("lat")
    me = g * 32 + a
    levels, lon = own_ref.shape[1:]
    loads = [
        pltpu.make_async_copy(src, dst, load_sems.at[n])
        for n, (src, dst) in enumerate(
            (
                (row_hbm, row_ref), (col_hbm, col_ref), (rw_hbm, rw_ref), (cw_hbm, cw_ref),
                (legendre_hbm, legendre_ref), (place_hbm, place_ref),
            )
        )
    ]
    for load in loads:
        load.start()

    barrier = pltpu.get_barrier_semaphore()
    following = lax.rem(me + 1, 256)
    previous = lax.rem(me + 255, 256)
    for other in (following, previous):
        pl.semaphore_signal(
            barrier, inc=1, device_id=(other // 32, lax.rem(other, 32)), device_id_type=MESH
        )

    @pl.loop(1, 32)
    def _(k):
        pl.semaphore_signal(
            barrier, inc=1, device_id=(g, lax.rem(a + k, 32)), device_id_type=MESH
        )

    @pl.loop(1, 8)
    def _(k):
        pl.semaphore_signal(
            barrier, inc=1, device_id=(lax.rem(g + k, 8), a), device_id_type=MESH
        )

    for i in range(2):
        sources[2 + i] = own_ref[i].astype(F32)
    fold = wave_table(slot_waves(wave_tile_ref[...]), table, lon)

    pl.semaphore_wait(barrier, 40)

    halo = [
        pltpu.make_async_remote_copy(
            src_ref=own_ref, dst_ref=target, send_sem=halo_send.at[n], recv_sem=halo_recv.at[n],
            device_id=(other // 32, lax.rem(other, 32)), device_id_type=MESH,
        )
        for n, (other, target) in enumerate(((following, before), (previous, after)))
    ]
    for move in halo:
        move.start()

    core, chip = lax.rem(a, 2), a // 2

    def optics_rows(which):
        return pl.ds(pl.multiple_of((core * 16 + which) * levels, levels), levels)

    def optics_copy(k, peer, block):
        return pltpu.make_async_remote_copy(
            src_ref=optics_ref, dst_ref=optics_all.at[optics_rows(block)],
            send_sem=opt_send.at[k], recv_sem=opt_recv.at[k],
            device_id=(g, peer * 2 + core), device_id_type=MESH,
        )

    @pl.loop(1, 16)
    def _(k):
        optics_copy(k, lax.rem(chip + k, 16), chip).start()

    optics_all[optics_rows(chip), :] = optics_ref[...]
    temps = coarse_means(own_ref)

    def exchange(source, target, block, send_sems, recv_sems, count, mine, peer_of):
        def copy(k, peer, place):
            return pltpu.make_async_remote_copy(
                src_ref=source.at[pl.ds(pl.multiple_of(peer * block, block), block)],
                dst_ref=target.at[pl.ds(pl.multiple_of(place * block, block), block)],
                send_sem=send_sems.at[k], recv_sem=recv_sems.at[k],
                device_id=peer_of(peer), device_id_type=MESH,
            )

        @pl.loop(1, count)
        def _(k):
            copy(k, lax.rem(mine + k, count), mine).start()

        here = pl.ds(pl.multiple_of(mine * block, block), block)
        target[here, :] = source[here, :]

        def finish():
            @pl.loop(1, count)
            def _(k):
                peer = lax.rem(mine + count - k, count)
                copy(k, lax.rem(mine + k, count), mine).wait_send()
                copy(k, peer, peer).wait_recv()

        return finish

    def over_lat(peer):
        return (g, peer)

    def over_grp(peer):
        return (peer, a)

    for load in loads[:4]:
        load.wait()
    for move in halo:
        move.wait_send()
        move.wait_recv()
    for i in range(2):
        sources[i] = before[i].astype(F32)
        sources[4 + i] = after[i].astype(F32)
    interpolate(2 * me, sources, row_ref, col_ref, rw_ref, cw_ref, departed)
    forward_waves(departed, z_ref, table, fold, ft_ref, sent)

    done = exchange(sent, got1, 16, send_lat, recv_lat, 32, a, over_lat)
    to_group = one_hot((512, 512), lat_first)

    @pl.loop(1, 16)
    def _(k):
        optics_copy(k, lax.rem(chip + k, 16), chip).wait_send()
        optics_copy(k, chip, lax.rem(chip + 16 - k, 16)).wait_recv()

    def relay_copy(which):
        half = optics_all.at[pl.ds(pl.multiple_of(which * (16 * levels), 16 * levels), 16 * levels)]
        return pltpu.make_async_remote_copy(
            src_ref=half, dst_ref=half, send_sem=relay_send.at[0], recv_sem=relay_recv.at[0],
            device_id=(g, chip * 2 + 1 - core), device_id_type=MESH,
        )

    relay_copy(core).start()
    done()
    send2[...] = permuted(to_group, got1[...]).astype(BF16)
    done = exchange(send2, got2, 64, send_grp, recv_grp, 8, g, over_grp)
    turn = (
        one_hot((256, 256), natural),
        one_hot((256, 256), lambda row: natural(255 - row)),
        one_hot((256, 256), unnatural),
        one_hot((256, 256), lambda row: 255 - unnatural(row)),
    )
    gamma = level_column(gamma_ref, 2 * levels)
    loads[4].wait()
    done()
    north, south = legendre_step(
        got2[0:256, :], got2[256:512, :], legendre_ref, gamma, waves_ref, me * 4, turn, trunc
    )
    send3[0:256, :] = north
    send3[256:512, :] = south
    done = exchange(send3, got3, 64, send_grp2, recv_grp2, 8, g, over_grp)
    to_lat = one_hot((512, 512), group_first)
    loads[5].wait()
    relay_copy(core).wait_send()
    relay_copy(1 - core).wait_recv()
    heat = radiate(
        temps, place_ref[...], optics_all, tall(kabs_ref[...]), tall(planck_ref[...]),
        kdown_ref[...],
    )
    done()
    send4[...] = permuted(to_lat, got3[...]).astype(BF16)
    done = exchange(send4, got4, 16, send_lat2, recv_lat2, 32, a, over_lat)
    heat = spread_heat(heat, lon)
    done()
    inverse_waves(got4, table, fold, heat, e_ref, out_ref)


def shards(
    state, dep_row, dep_col, row_weight, col_weight, wave_of, legendre, gamma,
    rad_place, optics, kabs, planck_weight, kdown,
):
    levels, lat_rows, lon = state.shape
    owners = lax.axis_size("lat")
    groups = lax.axis_size("grp")
    trunc = wave_of.shape[0] - 1
    coarse = lon // 4
    rows = 2 * groups * owners
    own = jnp.transpose(state, (1, 0, 2))
    in_vmem = pl.BlockSpec(memory_space=pltpu.VMEM)
    in_smem = pl.BlockSpec(memory_space=pltpu.SMEM)
    in_hbm = pl.BlockSpec(memory_space=pl.ANY)
    dma = pltpu.SemaphoreType.DMA
    result = pl.pallas_call(
        functools.partial(step_kernel, trunc),
        out_shape=jax.ShapeDtypeStruct((lat_rows, levels, lon), BF16),
        in_specs=[
            in_vmem, in_hbm, in_hbm, in_hbm, in_hbm, in_smem, in_vmem, in_hbm,
            in_smem, in_hbm, in_vmem, in_vmem, in_vmem, in_vmem,
        ],
        out_specs=in_vmem,
        scratch_shapes=[
            pltpu.VMEM((lat_rows, lon), jnp.int32),
            pltpu.VMEM((lat_rows, lon), jnp.int32),
            pltpu.VMEM((lat_rows, lon), F32),
            pltpu.VMEM((lat_rows, lon), F32),
            pltpu.VMEM(legendre.shape, BF16),
            pltpu.VMEM((1, coarse), jnp.int32),
            pltpu.VMEM((lat_rows, levels, lon), BF16),
            pltpu.VMEM((lat_rows, levels, lon), BF16),
            pltpu.VMEM((6, levels, lon), F32),
            pltpu.VMEM((2, levels, lon), F32),
            pltpu.VMEM((2048, 256), BF16),
            pltpu.VMEM((HALF * 2 * levels, 256), BF16),
            pltpu.VMEM((256, 256), F32),
            pltpu.VMEM((HALF * 2 * levels, 2048), BF16),
            pltpu.VMEM((owners * levels, coarse), BF16),
        ]
        + [pltpu.VMEM((rows, 128), BF16)] * 8
        + [dma((6,)), dma((2,)), dma((2,)), dma((16,)), dma((16,)), dma((1,)), dma((1,))]
        + [dma((32,)), dma((32,)), dma((8,)), dma((8,))]
        + [dma((8,)), dma((8,)), dma((32,)), dma((32,))],
        compiler_params=pltpu.CompilerParams(
            vmem_limit_bytes=VMEM_LIMIT, collective_id=0, has_side_effects=True
        ),
        name="model_step",
    )(
        own, dep_row, dep_col, row_weight, col_weight, wave_of,
        wave_of.reshape(groups, owners * 4), legendre, gamma, rad_place,
        jnp.transpose(optics), kabs, planck_weight, jnp.transpose(kdown),
    )
    return jnp.transpose(result, (1, 0, 2))


def solution(mesh):
    return jax.shard_map(
        shards,
        mesh=mesh,
        in_specs=(
            P(None, ("grp", "lat"), None),
            P(("grp", "lat"), None),
            P(("grp", "lat"), None),
            P(("grp", "lat"), None),
            P(("grp", "lat"), None),
            P(),
            P(("grp", "lat"), None, None, None),
            P(),
            P(("grp", "lat"), None),
            P(("grp", "lat"), None),
            P(),
            P(),
            P(),
        ),
        out_specs=P(None, ("grp", "lat"), None),
        check_vma=False,
    )
```

```python
import functools
import math

import jax
import jax.numpy as jnp
from jax import lax
from jax.experimental import pallas as pl
from jax.experimental.pallas import tpu as pltpu
from jax.sharding import PartitionSpec as P

F32 = jnp.float32
BF16 = jnp.bfloat16
RADIX = 32
HALF = RADIX // 2 + 1
VMEM_LIMIT = 62 * 1024 * 1024
MESH = pl.DeviceIdType.MESH
LAT_STEPS = [8 * y + 2 * x + c for y in (2, 1, 3, 0) for x in (2, 1, 3, 0) for c in (1, 0)]


def cplx(angle_num, angle_den):
    turn = 2.0 * math.pi * angle_num / angle_den
    return math.cos(turn), math.sin(turn)


def real_fft(planes):
    count = len(planes)
    if count == 2:
        return [(planes[0] + planes[1], None), (planes[0] - planes[1], None)]
    even = real_fft(planes[0::2])
    odd = real_fft(planes[1::2])
    half = count // 2
    out = []
    for k in range(half + 1):

        def pick(spec):
            kk = k % half
            if kk <= half // 2:
                return spec[kk]
            re, im = spec[half - kk]
            return re, (None if im is None else -im)

        er, ei = pick(even)
        orr, oi = pick(odd)
        c, s = cplx(k, count)
        if k == 0:
            out.append((er + orr, None))
        elif k == half:
            out.append((er - orr, None))
        elif 4 * k == count:
            out.append((er, -orr))
        else:
            if oi is None:
                tr, ti = c * orr, -s * orr
            else:
                tr, ti = c * orr + s * oi, c * oi - s * orr
            out.append((er + tr, ti if ei is None else ei + ti))
    return out


def real_ifft(spec):
    half = len(spec) - 1
    count = 2 * half
    if count == 2:
        return [spec[0][0] + spec[1][0], spec[0][0] - spec[1][0]]
    even, odd = [], []
    for k in range(half // 2 + 1):
        xr, xi = spec[k]
        yr, yi = spec[half - k]
        if k == 0:
            even.append((xr + yr, None))
            odd.append((xr - yr, None))
        elif 2 * k == half:
            even.append((xr + xr, None))
            odd.append((-(xi + xi), None))
        else:
            even.append((xr + yr, xi - yi))
            dr, di = xr - yr, xi + yi
            c, s = cplx(k, count)
            odd.append((c * dr - s * di, c * di + s * dr))
    ev, od = real_ifft(even), real_ifft(odd)
    return [plane for pair in zip(ev, od) for plane in pair]


def one_hot(shape, want):
    rows = lax.broadcasted_iota(jnp.int32, shape, 0)
    cols = lax.broadcasted_iota(jnp.int32, shape, 1)
    return jnp.where(want(rows) == cols, 1.0, 0.0).astype(BF16)


def permuted(matrix, data):
    return jnp.dot(matrix, data, preferred_element_type=F32)


def legendre_step(north_in, south_in, table_ref, gamma, waves_ref, first, turn, trunc):
    north = north_in.astype(F32)
    south = permuted(turn, south_in)
    sym = jnp.transpose(north + south).astype(BF16)
    anti = jnp.transpose(north - south).astype(BF16)
    half_degree = table_ref.shape[3]
    steps = lax.broadcasted_iota(jnp.int32, (1, half_degree), 1)
    norm = float(trunc * (trunc + 1))
    even_rows, odd_rows = [], []
    for s in range(4):
        pair = []
        for p, source in enumerate((sym, anti)):
            table = table_ref[s, p]
            spec = jnp.dot(source[32 * s : 32 * s + 32], table, preferred_element_type=F32)
            degree = (waves_ref[first + s] + 2 * steps + p).astype(F32)
            divisor = 1.0 + gamma * (degree * (degree + 1.0)) / norm
            solved = (spec / divisor).astype(BF16)
            pair.append(
                4.0
                * lax.dot_general(
                    solved, table, (((1,), (1,)), ((), ())), preferred_element_type=F32
                )
            )
        even_rows.append(pair[0])
        odd_rows.append(pair[1])
    even = jnp.concatenate(even_rows, axis=0)
    odd = jnp.concatenate(odd_rows, axis=0)
    north = jnp.transpose(even + odd).astype(BF16)
    south = jnp.transpose(even - odd).astype(BF16)
    return north, permuted(turn, south).astype(BF16)


def interpolate(start, sources, row_ref, col_ref, rw_ref, cw_ref, departed_ref):
    levels, lon = departed_ref.shape[1:]
    sub = lax.broadcasted_iota(jnp.int32, (8, lon), 0) - 2
    lon_ids = lax.broadcasted_iota(jnp.int32, (1, lon), 1)
    for i in range(2):
        rel_row = row_ref[i : i + 1, :] - (start + i)
        rel_col = ((col_ref[i : i + 1, :] - lon_ids + 2) & (lon - 1)) - 2
        a = rw_ref[i : i + 1, :]
        b = cw_ref[i : i + 1, :]
        row_w = jnp.where(rel_row == sub, 1.0 - a, 0.0) + jnp.where(rel_row == sub - 1, a, 0.0)
        col_w = jnp.where(rel_col == sub, 1.0 - b, 0.0) + jnp.where(rel_col == sub - 1, b, 0.0)
        shifted = [
            row_w if dc == 0 else pltpu.roll(row_w, dc % lon, 1) for dc in range(-2, 4)
        ]
        for h in range(levels // 8):
            total = None
            for dc in range(-2, 4):
                mixed = None
                for dr in range(5):
                    term = shifted[dc + 2][dr : dr + 1, :] * sources[i + dr, 8 * h : 8 * h + 8, :]
                    mixed = term if mixed is None else mixed + term
                if dc != 0:
                    mixed = pltpu.roll(mixed, (-dc) % lon, 1)
                term = col_w[dc + 2 : dc + 3, :] * mixed
                total = term if total is None else total + term
            departed_ref[i, 8 * h : 8 * h + 8, :] = total


def forward_waves(departed_ref, z_ref, tall_ref, fold, ft_ref, mix_ref, out_ref):
    levels, lon = departed_ref.shape[1:]
    for i in range(2):
        planes = [
            departed_ref[i, :, 128 * j : 128 * j + 128].astype(BF16).astype(F32)
            for j in range(RADIX)
        ]
        for k, (re, im) in enumerate(real_fft(planes)):
            at = 2 * levels * k + levels * i
            z_ref[at : at + levels, 0:128] = re.astype(BF16)
            z_ref[at : at + levels, 128:256] = (
                jnp.zeros((levels, 128), BF16) if im is None else im.astype(BF16)
            )
    scale = math.sqrt(2.0 / lon)
    r = 2 * levels
    for c in range(8):
        prod = jnp.dot(z_ref[...], tall_ref[c], preferred_element_type=F32)
        got = prod[0:r]
        for k in range(1, HALF):
            got = jnp.where(fold[c // 2] == k, prod[r * k : r * k + r], got)
        got = got * scale
        for i in range(2):
            ft_ref[128 * i + 16 * c : 128 * i + 16 * c + 16, :] = got[16 * i : 16 * i + 16]
    swapped = jnp.transpose(ft_ref[...])
    for i in range(2):
        mix_ref[pl.ds(i, 256, stride=2), :] = swapped[:, 128 * i : 128 * i + 128]
    out_ref[...] = mix_ref[...].astype(BF16).reshape(256, 2, 128)


def inverse_waves(got_ref, table_ref, fold, heat, e_ref, mix_ref, out_ref):
    levels, lon = out_ref.shape[1:]
    r = 2 * levels
    mix_ref[...] = got_ref[...].reshape(512, 128).astype(F32)
    turned = [jnp.transpose(mix_ref[pl.ds(i, 256, stride=2), :]) for i in range(2)]
    for c in range(8):
        piece = jnp.concatenate([t[16 * c : 16 * c + 16] for t in turned], axis=0)
        for k in range(HALF):
            e_ref[r * k : r * k + r, 256 * c : 256 * c + 256] = jnp.where(
                fold[c // 2] == k, piece, 0.0
            ).astype(BF16)
    waves = jnp.dot(e_ref[...], table_ref[...], preferred_element_type=F32)
    scale = 0.5 * math.sqrt(2.0 / lon)
    for i in range(2):
        spec = []
        for k in range(HALF):
            at = r * k + levels * i
            block = waves[at : at + levels]
            re, im = block[:, 0:128], block[:, 128:256]
            if k in (0, HALF - 1):
                spec.append((re + re, None))
            else:
                spec.append((re, im))
        for j, plane in enumerate(real_ifft(spec)):
            warm = heat[:, 128 * j : 128 * j + 128]
            out_ref[i, :, 128 * j : 128 * j + 128] = (plane * scale + warm).astype(BF16)


def coarse_means(own_ref):
    lon = own_ref.shape[2]
    high = lax.broadcasted_iota(jnp.int32, (512, 128), 0)
    low = lax.broadcasted_iota(jnp.int32, (512, 128), 1)
    pool = jnp.where(high // 4 == low, 1.0, 0.0).astype(BF16)
    temps = []
    for b in range(lon // 512):
        part = None
        for e in range(2):
            term = jnp.dot(
                own_ref[e, :, 512 * b : 512 * b + 512], pool, preferred_element_type=F32
            )
            part = term if part is None else part + term
        temps.append(part)
    return (jnp.concatenate(temps, axis=1) * 0.125).astype(BF16).astype(F32)


def radiate(temps, place, optics_ref, kabs, planck, kdown):
    levels, cols = temps.shape
    slot = place & (cols - 1)
    owner = place // cols
    block = (owner & 1) * 16 + owner // 2
    depth_all = None
    for b in range(cols // 256):
        ids = lax.broadcasted_iota(jnp.int32, (256, cols), 0) + 256 * b
        hot = jnp.where(ids == slot, 1.0, 0.0).astype(BF16)
        term = jnp.dot(
            optics_ref[:, 256 * b : 256 * b + 256], hot, preferred_element_type=F32
        )
        depth_all = term if depth_all is None else depth_all + term
    depth = depth_all[0:levels]
    for o in range(1, optics_ref.shape[0] // levels):
        depth = jnp.where(block == o, depth_all[levels * o : levels * o + levels], depth)
    best = lax.Precision.HIGHEST
    emission = 1.0 + jnp.tanh(temps)
    optical = jnp.dot(kabs, depth, precision=best, preferred_element_type=F32)
    source = jnp.dot(planck, emission, precision=best, preferred_element_type=F32)
    return jnp.dot(
        kdown, jnp.exp(-optical) * source, precision=best, preferred_element_type=F32
    ).astype(BF16)


def spread_heat(heat, lon):
    low = lax.broadcasted_iota(jnp.int32, (128, 512), 0)
    high = lax.broadcasted_iota(jnp.int32, (128, 512), 1)
    spread = jnp.where(low == high // 4, 1.0, 0.0).astype(BF16)
    return jnp.concatenate(
        [
            jnp.dot(heat[:, 128 * b : 128 * b + 128], spread, preferred_element_type=F32)
            for b in range(lon // 512)
        ],
        axis=1,
    )


def slot_waves(wave_tile):
    lane = lax.broadcasted_iota(jnp.int32, (128, 1024), 0)
    spot = lax.broadcasted_iota(jnp.int32, (128, 1024), 1)
    pick = jnp.where(lane == 4 * (spot & 31) + spot // 256, 1.0, 0.0).astype(BF16)
    high = (wave_tile // 32).astype(F32).astype(BF16)
    low = (wave_tile & 31).astype(F32).astype(BF16)
    spread = 32.0 * jnp.dot(high, pick, preferred_element_type=F32) + jnp.dot(
        low, pick, preferred_element_type=F32
    )
    group = lax.broadcasted_iota(jnp.int32, (8, 1024), 0)
    spot = lax.broadcasted_iota(jnp.int32, (8, 1024), 1)
    flat = jnp.sum(jnp.where(group == (spot & 255) // 32, spread, 0.0), axis=0, keepdims=True)
    return [flat[:, 256 * s : 256 * s + 256] for s in range(4)]


def turn_values(wave, step, lon):
    quarter = lon // 4
    point = (wave * step) & (lon - 1)
    turn = (point + quarter // 2) // quarter
    x = (point - turn * quarter).astype(F32) * (2.0 * math.pi / lon)
    y = x * x
    cosine = 1.0 + y * (-0.5 + y * (1.0 / 24 + y * (-1.0 / 720 + y * (1.0 / 40320))))
    sine = x * (1.0 + y * (-1.0 / 6 + y * (1.0 / 120 + y * (-1.0 / 5040 + y / 362880))))
    swap = (turn & 1) == 1
    c = jnp.where(swap, sine, cosine)
    n = jnp.where(swap, cosine, sine)
    c = jnp.where(((turn + 1) & 2) == 2, -c, c)
    n = jnp.where((turn & 2) == 2, -n, n)
    side = jnp.where((wave & (RADIX - 1)) > RADIX // 2, -1.0, 1.0)
    return c.astype(BF16), (side * n).astype(BF16), (-n).astype(BF16), (side * c).astype(BF16)


def fold_of(rows):
    fold = []
    for row in rows:
        kind = row.astype(jnp.int32) & (RADIX - 1)
        fold.append(jnp.minimum(kind, RADIX - kind))
    return fold


def tall_table(rows, tall_ref, lon):
    step = lax.broadcasted_iota(jnp.int32, (128, 256), 0)
    for s in range(4):
        a, b, c, d = turn_values(rows[s].astype(jnp.int32), step, lon)
        tall_ref[2 * s, 0:128, :] = a
        tall_ref[2 * s, 128:256, :] = b
        tall_ref[2 * s + 1, 0:128, :] = c
        tall_ref[2 * s + 1, 128:256, :] = d


def wide_table(rows, table_ref, lon):
    columns = jnp.transpose(jnp.concatenate(rows + [jnp.zeros((124, 256), F32)], axis=0))
    step = lax.broadcasted_iota(jnp.int32, (256, 128), 1)
    for s in range(4):
        a, b, c, d = turn_values(columns[:, s : s + 1].astype(jnp.int32), step, lon)
        at = 512 * s
        table_ref[at : at + 256, 0:128] = a
        table_ref[at : at + 256, 128:256] = b
        table_ref[at + 256 : at + 512, 0:128] = c
        table_ref[at + 256 : at + 512, 128:256] = d


def level_column(gamma_ref, rows):
    at = lax.broadcasted_iota(jnp.int32, (rows, 1), 0)
    levels = gamma_ref.shape[0]
    column = jnp.zeros((rows, 1), F32)
    for l in range(levels):
        column = jnp.where(at % levels == l, gamma_ref[l], column)
    return column


def tall(matrix):
    return jnp.transpose(jnp.concatenate([matrix, jnp.zeros((112, 128), F32)], axis=0))[:, 0:16]


def step_kernel(
    trunc, own_ref, row_hbm, col_hbm, rw_hbm, cw_hbm, waves_ref, wave_tile_hbm, legendre_hbm,
    gamma_ref, place_hbm, optics_hbm, kabs_hbm, planck_hbm, kdown_hbm, out_ref,
    row_ref, col_ref, rw_ref, cw_ref, wave_tile_ref, legendre_ref, place_ref, optics_ref,
    kabs_ref, planck_ref, kdown_ref,
    before, after, sources, departed, table, tall_ref, z_ref, ft_ref, mix_ref, e_ref, optics_all,
    sent, got, answer, back,
    load_sems, halo_send, halo_recv, opt_send, opt_recv, relay_send, relay_recv,
    out_send, out_recv, back_send, back_recv, ready,
):
    g = lax.axis_index("grp")
    a = lax.axis_index("lat")
    me = g * 32 + a
    levels, lon = own_ref.shape[1:]
    moves = (
        (wave_tile_hbm, wave_tile_ref), (optics_hbm, optics_ref),
        (row_hbm, row_ref), (col_hbm, col_ref), (rw_hbm, rw_ref), (cw_hbm, cw_ref),
        (legendre_hbm, legendre_ref), (place_hbm, place_ref), (kabs_hbm, kabs_ref),
        (planck_hbm, planck_ref), (kdown_hbm, kdown_ref),
    )
    loads = [
        pltpu.make_async_copy(src, dst, load_sems.at[n]) for n, (src, dst) in enumerate(moves)
    ]
    for load in loads:
        load.start()

    barrier = pltpu.get_barrier_semaphore()
    following = lax.rem(me + 1, 256)
    previous = lax.rem(me + 255, 256)
    for other in (following, previous):
        pl.semaphore_signal(
            barrier, inc=1, device_id=(other // 32, lax.rem(other, 32)), device_id_type=MESH
        )

    @pl.loop(1, 32)
    def _(k):
        pl.semaphore_signal(
            barrier, inc=1, device_id=(g, lax.rem(a + k, 32)), device_id_type=MESH
        )

    @pl.loop(1, 8)
    def _(k):
        pl.semaphore_signal(
            barrier, inc=1, device_id=(lax.rem(g + k, 8), a), device_id_type=MESH
        )

    for i in range(2):
        sources[2 + i] = own_ref[i].astype(F32)
    loads[0].wait()
    rows = slot_waves(wave_tile_ref[...])
    fold = fold_of(rows)
    tall_table(rows, tall_ref, lon)
    loads[1].wait()

    pl.semaphore_wait(barrier, 40)

    halo = [
        pltpu.make_async_remote_copy(
            src_ref=own_ref, dst_ref=target, send_sem=halo_send.at[n], recv_sem=halo_recv.at[n],
            device_id=(other // 32, lax.rem(other, 32)), device_id_type=MESH,
        )
        for n, (other, target) in enumerate(((following, before), (previous, after)))
    ]
    for move in halo:
        move.start()

    @pl.loop(1, 8)
    def _(k):
        pl.semaphore_signal(
            ready, inc=1, device_id=(lax.rem(g + k, 8), a), device_id_type=MESH
        )

    core, chip = lax.rem(a, 2), a // 2

    def optics_rows(which):
        return pl.ds(pl.multiple_of((core * 16 + which) * levels, levels), levels)

    def optics_copy(k, peer, block):
        return pltpu.make_async_remote_copy(
            src_ref=optics_ref, dst_ref=optics_all.at[optics_rows(block)],
            send_sem=opt_send.at[k], recv_sem=opt_recv.at[k],
            device_id=(g, peer * 2 + core), device_id_type=MESH,
        )

    @pl.loop(1, 16)
    def _(k):
        optics_copy(k, lax.rem(chip + k, 16), chip).start()

    optics_all[optics_rows(chip), :] = optics_ref[...]
    temps = coarse_means(own_ref)
    wide_table(rows, table, lon)

    def exchange(source, target, send_sem, recv_sem):
        def send(z, lat):
            pltpu.make_async_remote_copy(
                src_ref=source.at[z * 32 + lat], dst_ref=target.at[me],
                send_sem=send_sem.at[0], recv_sem=recv_sem.at[0],
                device_id=(z, lat), device_id_type=MESH,
            ).start()

        @pl.loop(0, 7)
        def _(k):
            z = g ^ jnp.where(k < 4, 4 + k, 7 - k)
            for step in LAT_STEPS:
                send(z, a ^ step)

        for step in LAT_STEPS[:-1]:
            send(g, a ^ step)
        target[me] = source[me]
        return pltpu.make_async_remote_copy(
            src_ref=source.at[pl.ds(0, 255)], dst_ref=target.at[pl.ds(0, 255)],
            send_sem=send_sem.at[0], recv_sem=recv_sem.at[0],
            device_id=(lax.rem(g + 1, 8), a), device_id_type=MESH,
        )

    for load in loads[2:6]:
        load.wait()
    for move in halo:
        move.wait_recv()
    for i in range(2):
        sources[i] = before[i].astype(F32)
        sources[4 + i] = after[i].astype(F32)
    interpolate(2 * me, sources, row_ref, col_ref, rw_ref, cw_ref, departed)
    forward_waves(departed, z_ref, tall_ref, fold, ft_ref, mix_ref, sent)
    pl.semaphore_wait(ready, 7)

    outward = exchange(sent, got, out_send, out_recv)

    @pl.loop(1, 16)
    def _(k):
        optics_copy(k, lax.rem(chip + k, 16), chip).wait_send()
        optics_copy(k, chip, lax.rem(chip + 16 - k, 16)).wait_recv()

    def relay_copy(which):
        half = optics_all.at[pl.ds(pl.multiple_of(which * (16 * levels), 16 * levels), 16 * levels)]
        return pltpu.make_async_remote_copy(
            src_ref=half, dst_ref=half, send_sem=relay_send.at[0], recv_sem=relay_recv.at[0],
            device_id=(g, chip * 2 + 1 - core), device_id_type=MESH,
        )

    relay_copy(core).start()
    turn = one_hot((256, 256), lambda row: 255 - row)
    gamma = level_column(gamma_ref, 2 * levels)
    for load in loads[6:]:
        load.wait()
    relay_copy(1 - core).wait_recv()
    heat = radiate(
        temps, place_ref[...], optics_all, tall(kabs_ref[...]), tall(planck_ref[...]),
        kdown_ref[...],
    )
    outward.wait_recv()
    north, south = legendre_step(
        got[0:128].reshape(256, 128), got[128:256].reshape(256, 128), legendre_ref, gamma,
        waves_ref, me * 4, turn, trunc,
    )
    answer[0:128] = north.reshape(128, 2, 128)
    answer[128:256] = south.reshape(128, 2, 128)
    homeward = exchange(answer, back, back_send, back_recv)
    heat = spread_heat(heat, lon)
    homeward.wait_recv()
    inverse_waves(back, table, fold, heat, e_ref, mix_ref, out_ref)
    for move in halo:
        move.wait_send()
    relay_copy(core).wait_send()
    outward.wait_send()
    homeward.wait_send()


def shards(
    state, dep_row, dep_col, row_weight, col_weight, wave_of, legendre, gamma,
    rad_place, optics, kabs, planck_weight, kdown,
):
    levels, lat_rows, lon = state.shape
    owners = lax.axis_size("lat")
    groups = lax.axis_size("grp")
    trunc = wave_of.shape[0] - 1
    coarse = lon // 4
    own = jnp.transpose(state, (1, 0, 2))
    in_vmem = pl.BlockSpec(memory_space=pltpu.VMEM)
    in_smem = pl.BlockSpec(memory_space=pltpu.SMEM)
    in_hbm = pl.BlockSpec(memory_space=pltpu.HBM)
    dma = pltpu.SemaphoreType.DMA
    result = pl.pallas_call(
        functools.partial(step_kernel, trunc),
        out_shape=jax.ShapeDtypeStruct((lat_rows, levels, lon), BF16),
        in_specs=[
            in_vmem, in_hbm, in_hbm, in_hbm, in_hbm, in_smem, in_hbm, in_hbm,
            in_smem, in_hbm, in_hbm, in_hbm, in_hbm, in_hbm,
        ],
        out_specs=in_vmem,
        scratch_shapes=[
            pltpu.VMEM((lat_rows, lon), jnp.int32),
            pltpu.VMEM((lat_rows, lon), jnp.int32),
            pltpu.VMEM((lat_rows, lon), F32),
            pltpu.VMEM((lat_rows, lon), F32),
            pltpu.VMEM((groups, owners * 4), jnp.int32),
            pltpu.VMEM(legendre.shape, BF16),
            pltpu.VMEM((1, coarse), jnp.int32),
            pltpu.VMEM((levels, coarse), BF16),
            pltpu.VMEM((levels, 128), F32),
            pltpu.VMEM((levels, 128), F32),
            pltpu.VMEM((levels, 128), F32),
            pltpu.VMEM((lat_rows, levels, lon), BF16),
            pltpu.VMEM((lat_rows, levels, lon), BF16),
            pltpu.VMEM((6, levels, lon), F32),
            pltpu.VMEM((2, levels, lon), F32),
            pltpu.VMEM((2048, 256), BF16),
            pltpu.VMEM((8, 256, 256), BF16),
            pltpu.VMEM((HALF * 2 * levels, 256), BF16),
            pltpu.VMEM((256, 256), F32),
            pltpu.VMEM((512, 128), F32),
            pltpu.VMEM((HALF * 2 * levels, 2048), BF16),
            pltpu.VMEM((owners * levels, coarse), BF16),
        ]
        + [pltpu.VMEM((groups * owners, 2, 128), BF16)] * 4
        + [dma((11,)), dma((2,)), dma((2,)), dma((16,)), dma((16,)), dma((1,)), dma((1,))]
        + [dma((1,))] * 4
        + [pltpu.SemaphoreType.REGULAR],
        compiler_params=pltpu.CompilerParams(
            vmem_limit_bytes=VMEM_LIMIT, collective_id=0, has_side_effects=True
        ),
        name="model_step",
    )(
        own, dep_row, dep_col, row_weight, col_weight, wave_of,
        wave_of.reshape(groups, owners * 4), legendre, gamma, rad_place,
        jnp.transpose(optics), kabs, planck_weight, jnp.transpose(kdown),
    )
    return jnp.transpose(result, (1, 0, 2))


def solution(mesh):
    return jax.shard_map(
        shards,
        mesh=mesh,
        in_specs=(
            P(None, ("grp", "lat"), None),
            P(("grp", "lat"), None),
            P(("grp", "lat"), None),
            P(("grp", "lat"), None),
            P(("grp", "lat"), None),
            P(),
            P(("grp", "lat"), None, None, None),
            P(),
            P(("grp", "lat"), None),
            P(("grp", "lat"), None),
            P(),
            P(),
            P(),
        ),
        out_specs=P(None, ("grp", "lat"), None),
        check_vma=False,
    )
```

```python
import functools
import math

import jax
import jax.numpy as jnp
from jax import lax
from jax.experimental import pallas as pl
from jax.experimental.pallas import tpu as pltpu
from jax.sharding import PartitionSpec as P

F32 = jnp.float32
BF16 = jnp.bfloat16
RADIX = 32
HALF = RADIX // 2 + 1
VMEM_LIMIT = 62 * 1024 * 1024
MESH = pl.DeviceIdType.MESH
LAT_STEPS = [8 * y + 2 * x + c for y in (2, 1, 3, 0) for x in (2, 1, 3, 0) for c in (1, 0)]


def cplx(angle_num, angle_den):
    turn = 2.0 * math.pi * angle_num / angle_den
    return math.cos(turn), math.sin(turn)


def real_fft(planes):
    count = len(planes)
    if count == 2:
        return [(planes[0] + planes[1], None), (planes[0] - planes[1], None)]
    even = real_fft(planes[0::2])
    odd = real_fft(planes[1::2])
    half = count // 2
    out = []
    for k in range(half + 1):

        def pick(spec):
            kk = k % half
            if kk <= half // 2:
                return spec[kk]
            re, im = spec[half - kk]
            return re, (None if im is None else -im)

        er, ei = pick(even)
        orr, oi = pick(odd)
        c, s = cplx(k, count)
        if k == 0:
            out.append((er + orr, None))
        elif k == half:
            out.append((er - orr, None))
        elif 4 * k == count:
            out.append((er, -orr))
        else:
            if oi is None:
                tr, ti = c * orr, -s * orr
            else:
                tr, ti = c * orr + s * oi, c * oi - s * orr
            out.append((er + tr, ti if ei is None else ei + ti))
    return out


def real_ifft(spec):
    half = len(spec) - 1
    count = 2 * half
    if count == 2:
        return [spec[0][0] + spec[1][0], spec[0][0] - spec[1][0]]
    even, odd = [], []
    for k in range(half // 2 + 1):
        xr, xi = spec[k]
        yr, yi = spec[half - k]
        if k == 0:
            even.append((xr + yr, None))
            odd.append((xr - yr, None))
        elif 2 * k == half:
            even.append((xr + xr, None))
            odd.append((-(xi + xi), None))
        else:
            even.append((xr + yr, xi - yi))
            dr, di = xr - yr, xi + yi
            c, s = cplx(k, count)
            odd.append((c * dr - s * di, c * di + s * dr))
    ev, od = real_ifft(even), real_ifft(odd)
    return [plane for pair in zip(ev, od) for plane in pair]


def one_hot(shape, want):
    rows = lax.broadcasted_iota(jnp.int32, shape, 0)
    cols = lax.broadcasted_iota(jnp.int32, shape, 1)
    return jnp.where(want(rows) == cols, 1.0, 0.0).astype(BF16)


def permuted(matrix, data):
    return jnp.dot(matrix, data, preferred_element_type=F32)


def legendre_step(north_in, south_in, table_ref, gamma, waves_ref, first, turn, trunc):
    north = north_in.astype(F32)
    south = permuted(turn, south_in)
    sym = jnp.transpose(north + south).astype(BF16)
    anti = jnp.transpose(north - south).astype(BF16)
    half_degree = table_ref.shape[3]
    steps = lax.broadcasted_iota(jnp.int32, (1, half_degree), 1)
    norm = float(trunc * (trunc + 1))
    even_rows, odd_rows = [], []
    for s in range(4):
        pair = []
        for p, source in enumerate((sym, anti)):
            table = table_ref[s, p]
            spec = jnp.dot(source[32 * s : 32 * s + 32], table, preferred_element_type=F32)
            degree = (waves_ref[first + s] + 2 * steps + p).astype(F32)
            divisor = 1.0 + gamma * (degree * (degree + 1.0)) / norm
            solved = (spec / divisor).astype(BF16)
            pair.append(
                4.0
                * lax.dot_general(
                    solved, table, (((1,), (1,)), ((), ())), preferred_element_type=F32
                )
            )
        even_rows.append(pair[0])
        odd_rows.append(pair[1])
    even = jnp.concatenate(even_rows, axis=0)
    odd = jnp.concatenate(odd_rows, axis=0)
    north = jnp.transpose(even + odd).astype(BF16)
    south = jnp.transpose(even - odd).astype(BF16)
    return north, permuted(turn, south).astype(BF16)


def departure_weights(start, row_ref, col_ref, rw_ref, cw_ref, near_ref, col_w_ref, far_ref):
    lon = row_ref.shape[1]
    sub = lax.broadcasted_iota(jnp.int32, (8, lon), 0) - 2
    lon_ids = lax.broadcasted_iota(jnp.int32, (1, lon), 1)
    for i in range(2):
        rel_row = row_ref[i : i + 1, :] - (start + i)
        rel_col = ((col_ref[i : i + 1, :] - lon_ids + 2) & (lon - 1)) - 2
        a = rw_ref[i : i + 1, :]
        b = cw_ref[i : i + 1, :]
        row_w = jnp.where(rel_row == sub, 1.0 - a, 0.0) + jnp.where(rel_row == sub - 1, a, 0.0)
        col_w = jnp.where(rel_col == sub, 1.0 - b, 0.0) + jnp.where(rel_col == sub - 1, b, 0.0)
        for dc in range(-2, 4):
            near_ref[i, dc + 2] = row_w if dc == 0 else pltpu.roll(row_w, dc % lon, 1)
        col_w_ref[i] = col_w
        far_ref[i] = row_w[4 * i : 4 * i + 1, :] * col_w


def near_rows(sources, near_ref, col_w_ref, departed_ref):
    levels, lon = departed_ref.shape[1:]
    for i in range(2):
        for h in range(levels // 8):
            total = None
            for dc in range(-2, 4):
                mixed = None
                for dr in range(1 - i, 5 - i):
                    term = (
                        near_ref[i, dc + 2, dr : dr + 1, :]
                        * sources[i + dr - 1, 8 * h : 8 * h + 8, :]
                    )
                    mixed = term if mixed is None else mixed + term
                if dc != 0:
                    mixed = pltpu.roll(mixed, (-dc) % lon, 1)
                term = col_w_ref[i, dc + 2 : dc + 3, :] * mixed
                total = term if total is None else total + term
            departed_ref[i, 8 * h : 8 * h + 8, :] = total


def far_rows(rows, far_ref, departed_ref):
    levels, lon = departed_ref.shape[1:]
    for i in range(2):
        for h in range(levels // 8):
            source = rows[i][8 * h : 8 * h + 8, :].astype(F32)
            total = departed_ref[i, 8 * h : 8 * h + 8, :]
            for dc in range(-2, 4):
                moved = source if dc == 0 else pltpu.roll(source, (-dc) % lon, 1)
                total = total + far_ref[i, dc + 2 : dc + 3, :] * moved
            departed_ref[i, 8 * h : 8 * h + 8, :] = total


def forward_waves(departed_ref, z_ref, tall_ref, fold, ft_ref, mix_ref, out_ref):
    levels, lon = departed_ref.shape[1:]
    for i in range(2):
        planes = [
            departed_ref[i, :, 128 * j : 128 * j + 128].astype(BF16).astype(F32)
            for j in range(RADIX)
        ]
        for k, (re, im) in enumerate(real_fft(planes)):
            at = 2 * levels * k + levels * i
            z_ref[at : at + levels, 0:128] = re.astype(BF16)
            z_ref[at : at + levels, 128:256] = (
                jnp.zeros((levels, 128), BF16) if im is None else im.astype(BF16)
            )
    scale = math.sqrt(2.0 / lon)
    r = 2 * levels
    for c in range(8):
        prod = jnp.dot(z_ref[...], tall_ref[c], preferred_element_type=F32)
        got = prod[0:r]
        for k in range(1, HALF):
            got = jnp.where(fold[c // 2] == k, prod[r * k : r * k + r], got)
        got = got * scale
        for i in range(2):
            ft_ref[128 * i + 16 * c : 128 * i + 16 * c + 16, :] = got[16 * i : 16 * i + 16]
    swapped = jnp.transpose(ft_ref[...])
    for i in range(2):
        mix_ref[pl.ds(i, 256, stride=2), :] = swapped[:, 128 * i : 128 * i + 128]
    out_ref[...] = mix_ref[...].astype(BF16).reshape(256, 2, 128)


def inverse_waves(got_ref, table_ref, fold, heat, e_ref, mix_ref, out_ref):
    levels, lon = out_ref.shape[1:]
    r = 2 * levels
    mix_ref[...] = got_ref[...].reshape(512, 128).astype(F32)
    turned = [jnp.transpose(mix_ref[pl.ds(i, 256, stride=2), :]) for i in range(2)]
    for c in range(8):
        piece = jnp.concatenate([t[16 * c : 16 * c + 16] for t in turned], axis=0)
        for k in range(HALF):
            e_ref[r * k : r * k + r, 256 * c : 256 * c + 256] = jnp.where(
                fold[c // 2] == k, piece, 0.0
            ).astype(BF16)
    waves = jnp.dot(e_ref[...], table_ref[...], preferred_element_type=F32)
    scale = 0.5 * math.sqrt(2.0 / lon)
    for i in range(2):
        spec = []
        for k in range(HALF):
            at = r * k + levels * i
            block = waves[at : at + levels]
            re, im = block[:, 0:128], block[:, 128:256]
            if k in (0, HALF - 1):
                spec.append((re + re, None))
            else:
                spec.append((re, im))
        for j, plane in enumerate(real_ifft(spec)):
            warm = heat[:, 128 * j : 128 * j + 128]
            out_ref[i, :, 128 * j : 128 * j + 128] = (plane * scale + warm).astype(BF16)


def coarse_means(own_ref):
    lon = own_ref.shape[2]
    high = lax.broadcasted_iota(jnp.int32, (512, 128), 0)
    low = lax.broadcasted_iota(jnp.int32, (512, 128), 1)
    pool = jnp.where(high // 4 == low, 1.0, 0.0).astype(BF16)
    temps = []
    for b in range(lon // 512):
        part = None
        for e in range(2):
            term = jnp.dot(
                own_ref[e, :, 512 * b : 512 * b + 512], pool, preferred_element_type=F32
            )
            part = term if part is None else part + term
        temps.append(part)
    return (jnp.concatenate(temps, axis=1) * 0.125).astype(BF16).astype(F32)


def radiate(temps, place, optics_ref, kabs, planck, kdown):
    levels, cols = temps.shape
    slot = place & (cols - 1)
    owner = place // cols
    block = (owner & 1) * 16 + owner // 2
    depth_all = None
    for b in range(cols // 256):
        ids = lax.broadcasted_iota(jnp.int32, (256, cols), 0) + 256 * b
        hot = jnp.where(ids == slot, 1.0, 0.0).astype(BF16)
        term = jnp.dot(
            optics_ref[:, 256 * b : 256 * b + 256], hot, preferred_element_type=F32
        )
        depth_all = term if depth_all is None else depth_all + term
    depth = depth_all[0:levels]
    for o in range(1, optics_ref.shape[0] // levels):
        depth = jnp.where(block == o, depth_all[levels * o : levels * o + levels], depth)
    best = lax.Precision.HIGHEST
    emission = 1.0 + jnp.tanh(temps)
    optical = jnp.dot(kabs, depth, precision=best, preferred_element_type=F32)
    source = jnp.dot(planck, emission, precision=best, preferred_element_type=F32)
    return jnp.dot(
        kdown, jnp.exp(-optical) * source, precision=best, preferred_element_type=F32
    ).astype(BF16)


def spread_heat(heat, lon):
    low = lax.broadcasted_iota(jnp.int32, (128, 512), 0)
    high = lax.broadcasted_iota(jnp.int32, (128, 512), 1)
    spread = jnp.where(low == high // 4, 1.0, 0.0).astype(BF16)
    return jnp.concatenate(
        [
            jnp.dot(heat[:, 128 * b : 128 * b + 128], spread, preferred_element_type=F32)
            for b in range(lon // 512)
        ],
        axis=1,
    )


def slot_waves(wave_tile):
    lane = lax.broadcasted_iota(jnp.int32, (128, 1024), 0)
    spot = lax.broadcasted_iota(jnp.int32, (128, 1024), 1)
    pick = jnp.where(lane == 4 * (spot & 31) + spot // 256, 1.0, 0.0).astype(BF16)
    high = (wave_tile // 32).astype(F32).astype(BF16)
    low = (wave_tile & 31).astype(F32).astype(BF16)
    spread = 32.0 * jnp.dot(high, pick, preferred_element_type=F32) + jnp.dot(
        low, pick, preferred_element_type=F32
    )
    group = lax.broadcasted_iota(jnp.int32, (8, 1024), 0)
    spot = lax.broadcasted_iota(jnp.int32, (8, 1024), 1)
    flat = jnp.sum(jnp.where(group == (spot & 255) // 32, spread, 0.0), axis=0, keepdims=True)
    return [flat[:, 256 * s : 256 * s + 256] for s in range(4)]


def turn_values(wave, step, lon):
    quarter = lon // 4
    point = (wave * step) & (lon - 1)
    turn = (point + quarter // 2) // quarter
    x = (point - turn * quarter).astype(F32) * (2.0 * math.pi / lon)
    y = x * x
    cosine = 1.0 + y * (-0.5 + y * (1.0 / 24 + y * (-1.0 / 720 + y * (1.0 / 40320))))
    sine = x * (1.0 + y * (-1.0 / 6 + y * (1.0 / 120 + y * (-1.0 / 5040 + y / 362880))))
    swap = (turn & 1) == 1
    c = jnp.where(swap, sine, cosine)
    n = jnp.where(swap, cosine, sine)
    c = jnp.where(((turn + 1) & 2) == 2, -c, c)
    n = jnp.where((turn & 2) == 2, -n, n)
    side = jnp.where((wave & (RADIX - 1)) > RADIX // 2, -1.0, 1.0)
    return c.astype(BF16), (side * n).astype(BF16), (-n).astype(BF16), (side * c).astype(BF16)


def fold_of(rows):
    fold = []
    for row in rows:
        kind = row.astype(jnp.int32) & (RADIX - 1)
        fold.append(jnp.minimum(kind, RADIX - kind))
    return fold


def tall_table(rows, tall_ref, lon):
    step = lax.broadcasted_iota(jnp.int32, (128, 256), 0)
    for s in range(4):
        a, b, c, d = turn_values(rows[s].astype(jnp.int32), step, lon)
        tall_ref[2 * s, 0:128, :] = a
        tall_ref[2 * s, 128:256, :] = b
        tall_ref[2 * s + 1, 0:128, :] = c
        tall_ref[2 * s + 1, 128:256, :] = d


def wide_table(rows, table_ref, lon):
    columns = jnp.transpose(jnp.concatenate(rows + [jnp.zeros((124, 256), F32)], axis=0))
    step = lax.broadcasted_iota(jnp.int32, (256, 128), 1)
    for s in range(4):
        a, b, c, d = turn_values(columns[:, s : s + 1].astype(jnp.int32), step, lon)
        at = 512 * s
        table_ref[at : at + 256, 0:128] = a
        table_ref[at : at + 256, 128:256] = b
        table_ref[at + 256 : at + 512, 0:128] = c
        table_ref[at + 256 : at + 512, 128:256] = d


def level_column(gamma_ref, rows):
    at = lax.broadcasted_iota(jnp.int32, (rows, 1), 0)
    levels = gamma_ref.shape[0]
    column = jnp.zeros((rows, 1), F32)
    for l in range(levels):
        column = jnp.where(at % levels == l, gamma_ref[l], column)
    return column


def tall(matrix):
    return jnp.transpose(jnp.concatenate([matrix, jnp.zeros((112, 128), F32)], axis=0))[:, 0:16]


def step_kernel(
    trunc, own_ref, row_hbm, col_hbm, rw_hbm, cw_hbm, waves_ref, wave_tile_hbm, legendre_hbm,
    gamma_ref, place_hbm, optics_hbm, kabs_hbm, planck_hbm, kdown_hbm, out_ref,
    row_ref, col_ref, rw_ref, cw_ref, wave_tile_ref, legendre_ref, place_ref, optics_ref,
    kabs_ref, planck_ref, kdown_ref,
    before, after, sources, near_ref, col_w_ref, far_ref, departed, table, tall_ref, z_ref, ft_ref, mix_ref, e_ref, optics_all,
    sent, got, answer, back,
    load_sems, halo_send, halo_recv, opt_send, opt_recv, relay_send, relay_recv,
    out_send, out_recv, back_send, back_recv, ready,
):
    g = lax.axis_index("grp")
    a = lax.axis_index("lat")
    me = g * 32 + a
    levels, lon = own_ref.shape[1:]
    moves = (
        (wave_tile_hbm, wave_tile_ref), (optics_hbm, optics_ref),
        (row_hbm, row_ref), (col_hbm, col_ref), (rw_hbm, rw_ref), (cw_hbm, cw_ref),
        (legendre_hbm, legendre_ref), (place_hbm, place_ref), (kabs_hbm, kabs_ref),
        (planck_hbm, planck_ref), (kdown_hbm, kdown_ref),
    )
    loads = [
        pltpu.make_async_copy(src, dst, load_sems.at[n]) for n, (src, dst) in enumerate(moves)
    ]
    for load in loads:
        load.start()

    barrier = pltpu.get_barrier_semaphore()
    following = lax.rem(me + 1, 256)
    previous = lax.rem(me + 255, 256)
    for other in (following, previous):
        pl.semaphore_signal(
            barrier, inc=1, device_id=(other // 32, lax.rem(other, 32)), device_id_type=MESH
        )

    @pl.loop(1, 32)
    def _(k):
        pl.semaphore_signal(
            barrier, inc=1, device_id=(g, lax.rem(a + k, 32)), device_id_type=MESH
        )

    @pl.loop(1, 8)
    def _(k):
        pl.semaphore_signal(
            barrier, inc=1, device_id=(lax.rem(g + k, 8), a), device_id_type=MESH
        )

    for i in range(2):
        sources[1 + i] = own_ref[i].astype(F32)
    loads[0].wait()
    rows = slot_waves(wave_tile_ref[...])
    fold = fold_of(rows)
    tall_table(rows, tall_ref, lon)
    loads[1].wait()

    pl.semaphore_wait(barrier, 40)

    def halo(n, row):
        other, target = ((following, before), (previous, after))[n]
        return pltpu.make_async_remote_copy(
            src_ref=own_ref.at[row], dst_ref=target.at[row],
            send_sem=halo_send.at[2 * n + row], recv_sem=halo_recv.at[2 * n + row],
            device_id=(other // 32, lax.rem(other, 32)), device_id_type=MESH,
        )

    near = (halo(0, 1), halo(1, 0))
    far = (halo(0, 0), halo(1, 1))
    for move in near + far:
        move.start()

    @pl.loop(1, 8)
    def _(k):
        pl.semaphore_signal(
            ready, inc=1, device_id=(lax.rem(g + k, 8), a), device_id_type=MESH
        )

    core, chip = lax.rem(a, 2), a // 2

    def optics_rows(which):
        return pl.ds(pl.multiple_of((core * 16 + which) * levels, levels), levels)

    def optics_copy(k, peer, block):
        return pltpu.make_async_remote_copy(
            src_ref=optics_ref, dst_ref=optics_all.at[optics_rows(block)],
            send_sem=opt_send.at[k], recv_sem=opt_recv.at[k],
            device_id=(g, peer * 2 + core), device_id_type=MESH,
        )

    optics_all[optics_rows(chip), :] = optics_ref[...]
    temps = coarse_means(own_ref)
    wide_table(rows, table, lon)

    def exchange(source, target, send_sem, recv_sem):
        def send(z, lat):
            pltpu.make_async_remote_copy(
                src_ref=source.at[z * 32 + lat], dst_ref=target.at[me],
                send_sem=send_sem.at[0], recv_sem=recv_sem.at[0],
                device_id=(z, lat), device_id_type=MESH,
            ).start()

        @pl.loop(0, 7)
        def _(k):
            z = g ^ jnp.where(k < 4, 4 + k, 7 - k)
            for step in LAT_STEPS:
                send(z, a ^ step)

        for step in LAT_STEPS[:-1]:
            send(g, a ^ step)
        target[me] = source[me]
        return pltpu.make_async_remote_copy(
            src_ref=source.at[pl.ds(0, 255)], dst_ref=target.at[pl.ds(0, 255)],
            send_sem=send_sem.at[0], recv_sem=recv_sem.at[0],
            device_id=(lax.rem(g + 1, 8), a), device_id_type=MESH,
        )

    for load in loads[2:6]:
        load.wait()
    departure_weights(
        2 * me, row_ref, col_ref, rw_ref, cw_ref, near_ref, col_w_ref, far_ref
    )
    for move in near:
        move.wait_recv()
    sources[0] = before[1].astype(F32)
    sources[3] = after[0].astype(F32)
    near_rows(sources, near_ref, col_w_ref, departed)
    for move in far:
        move.wait_recv()

    @pl.loop(1, 16)
    def _(k):
        optics_copy(k, lax.rem(chip + k, 16), chip).start()

    far_rows((before.at[0], after.at[1]), far_ref, departed)
    forward_waves(departed, z_ref, tall_ref, fold, ft_ref, mix_ref, sent)
    pl.semaphore_wait(ready, 7)

    outward = exchange(sent, got, out_send, out_recv)

    @pl.loop(1, 16)
    def _(k):
        optics_copy(k, lax.rem(chip + k, 16), chip).wait_send()
        optics_copy(k, chip, lax.rem(chip + 16 - k, 16)).wait_recv()

    def relay_copy(which):
        half = optics_all.at[pl.ds(pl.multiple_of(which * (16 * levels), 16 * levels), 16 * levels)]
        return pltpu.make_async_remote_copy(
            src_ref=half, dst_ref=half, send_sem=relay_send.at[0], recv_sem=relay_recv.at[0],
            device_id=(g, chip * 2 + 1 - core), device_id_type=MESH,
        )

    relay_copy(core).start()
    turn = one_hot((256, 256), lambda row: 255 - row)
    gamma = level_column(gamma_ref, 2 * levels)
    loads[6].wait()
    outward.wait_recv()
    north, south = legendre_step(
        got[0:128].reshape(256, 128), got[128:256].reshape(256, 128), legendre_ref, gamma,
        waves_ref, me * 4, turn, trunc,
    )
    answer[0:128] = north.reshape(128, 2, 128)
    answer[128:256] = south.reshape(128, 2, 128)
    homeward = exchange(answer, back, back_send, back_recv)
    for load in loads[7:]:
        load.wait()
    relay_copy(1 - core).wait_recv()
    heat = radiate(
        temps, place_ref[...], optics_all, tall(kabs_ref[...]), tall(planck_ref[...]),
        kdown_ref[...],
    )
    heat = spread_heat(heat, lon)
    homeward.wait_recv()
    inverse_waves(back, table, fold, heat, e_ref, mix_ref, out_ref)
    for move in near + far:
        move.wait_send()
    relay_copy(core).wait_send()
    outward.wait_send()
    homeward.wait_send()


def shards(
    state, dep_row, dep_col, row_weight, col_weight, wave_of, legendre, gamma,
    rad_place, optics, kabs, planck_weight, kdown,
):
    levels, lat_rows, lon = state.shape
    owners = lax.axis_size("lat")
    groups = lax.axis_size("grp")
    trunc = wave_of.shape[0] - 1
    coarse = lon // 4
    own = jnp.transpose(state, (1, 0, 2))
    in_vmem = pl.BlockSpec(memory_space=pltpu.VMEM)
    in_smem = pl.BlockSpec(memory_space=pltpu.SMEM)
    in_hbm = pl.BlockSpec(memory_space=pltpu.HBM)
    dma = pltpu.SemaphoreType.DMA
    result = pl.pallas_call(
        functools.partial(step_kernel, trunc),
        out_shape=jax.ShapeDtypeStruct((lat_rows, levels, lon), BF16),
        in_specs=[
            in_vmem, in_hbm, in_hbm, in_hbm, in_hbm, in_smem, in_hbm, in_hbm,
            in_smem, in_hbm, in_hbm, in_hbm, in_hbm, in_hbm,
        ],
        out_specs=in_vmem,
        scratch_shapes=[
            pltpu.VMEM((lat_rows, lon), jnp.int32),
            pltpu.VMEM((lat_rows, lon), jnp.int32),
            pltpu.VMEM((lat_rows, lon), F32),
            pltpu.VMEM((lat_rows, lon), F32),
            pltpu.VMEM((groups, owners * 4), jnp.int32),
            pltpu.VMEM(legendre.shape, BF16),
            pltpu.VMEM((1, coarse), jnp.int32),
            pltpu.VMEM((levels, coarse), BF16),
            pltpu.VMEM((levels, 128), F32),
            pltpu.VMEM((levels, 128), F32),
            pltpu.VMEM((levels, 128), F32),
            pltpu.VMEM((lat_rows, levels, lon), BF16),
            pltpu.VMEM((lat_rows, levels, lon), BF16),
            pltpu.VMEM((4, levels, lon), F32),
            pltpu.VMEM((2, 6, 8, lon), F32),
            pltpu.VMEM((2, 8, lon), F32),
            pltpu.VMEM((2, 8, lon), F32),
            pltpu.VMEM((2, levels, lon), F32),
            pltpu.VMEM((2048, 256), BF16),
            pltpu.VMEM((8, 256, 256), BF16),
            pltpu.VMEM((HALF * 2 * levels, 256), BF16),
            pltpu.VMEM((256, 256), F32),
            pltpu.VMEM((512, 128), F32),
            pltpu.VMEM((HALF * 2 * levels, 2048), BF16),
            pltpu.VMEM((owners * levels, coarse), BF16),
        ]
        + [pltpu.VMEM((groups * owners, 2, 128), BF16)] * 4
        + [dma((11,)), dma((4,)), dma((4,)), dma((16,)), dma((16,)), dma((1,)), dma((1,))]
        + [dma((1,))] * 4
        + [pltpu.SemaphoreType.REGULAR],
        compiler_params=pltpu.CompilerParams(
            vmem_limit_bytes=VMEM_LIMIT, collective_id=0, has_side_effects=True
        ),
        name="model_step",
    )(
        own, dep_row, dep_col, row_weight, col_weight, wave_of,
        wave_of.reshape(groups, owners * 4), legendre, gamma, rad_place,
        jnp.transpose(optics), kabs, planck_weight, jnp.transpose(kdown),
    )
    return jnp.transpose(result, (1, 0, 2))


def solution(mesh):
    return jax.shard_map(
        shards,
        mesh=mesh,
        in_specs=(
            P(None, ("grp", "lat"), None),
            P(("grp", "lat"), None),
            P(("grp", "lat"), None),
            P(("grp", "lat"), None),
            P(("grp", "lat"), None),
            P(),
            P(("grp", "lat"), None, None, None),
            P(),
            P(("grp", "lat"), None),
            P(("grp", "lat"), None),
            P(),
            P(),
            P(),
        ),
        out_specs=P(None, ("grp", "lat"), None),
        check_vma=False,
    )
```

```python
import functools
import math

import jax
import jax.numpy as jnp
from jax import lax
from jax.experimental import pallas as pl
from jax.experimental.pallas import tpu as pltpu
from jax.sharding import PartitionSpec as P

F32 = jnp.float32
BF16 = jnp.bfloat16
RADIX = 32
HALF = RADIX // 2 + 1
VMEM_LIMIT = 62 * 1024 * 1024
MESH = pl.DeviceIdType.MESH
LAT_STEPS = [8 * y + 2 * x + c for y in (2, 1, 3, 0) for x in (2, 1, 3, 0) for c in (1, 0)]


def cplx(angle_num, angle_den):
    turn = 2.0 * math.pi * angle_num / angle_den
    return math.cos(turn), math.sin(turn)


def real_fft(planes):
    count = len(planes)
    if count == 2:
        return [(planes[0] + planes[1], None), (planes[0] - planes[1], None)]
    even = real_fft(planes[0::2])
    odd = real_fft(planes[1::2])
    half = count // 2
    out = []
    for k in range(half + 1):

        def pick(spec):
            kk = k % half
            if kk <= half // 2:
                return spec[kk]
            re, im = spec[half - kk]
            return re, (None if im is None else -im)

        er, ei = pick(even)
        orr, oi = pick(odd)
        c, s = cplx(k, count)
        if k == 0:
            out.append((er + orr, None))
        elif k == half:
            out.append((er - orr, None))
        elif 4 * k == count:
            out.append((er, -orr))
        else:
            if oi is None:
                tr, ti = c * orr, -s * orr
            else:
                tr, ti = c * orr + s * oi, c * oi - s * orr
            out.append((er + tr, ti if ei is None else ei + ti))
    return out


def real_ifft(spec):
    half = len(spec) - 1
    count = 2 * half
    if count == 2:
        return [spec[0][0] + spec[1][0], spec[0][0] - spec[1][0]]
    even, odd = [], []
    for k in range(half // 2 + 1):
        xr, xi = spec[k]
        yr, yi = spec[half - k]
        if k == 0:
            even.append((xr + yr, None))
            odd.append((xr - yr, None))
        elif 2 * k == half:
            even.append((xr + xr, None))
            odd.append((-(xi + xi), None))
        else:
            even.append((xr + yr, xi - yi))
            dr, di = xr - yr, xi + yi
            c, s = cplx(k, count)
            odd.append((c * dr - s * di, c * di + s * dr))
    ev, od = real_ifft(even), real_ifft(odd)
    return [plane for pair in zip(ev, od) for plane in pair]


def one_hot(shape, want):
    rows = lax.broadcasted_iota(jnp.int32, shape, 0)
    cols = lax.broadcasted_iota(jnp.int32, shape, 1)
    return jnp.where(want(rows) == cols, 1.0, 0.0).astype(BF16)


def permuted(matrix, data):
    return jnp.dot(matrix, data, preferred_element_type=F32)


def legendre_step(north_in, south_in, table_ref, gamma, waves_ref, first, turn, trunc):
    north = north_in.astype(F32)
    south = permuted(turn, south_in)
    sym = jnp.transpose(north + south).astype(BF16)
    anti = jnp.transpose(north - south).astype(BF16)
    half_degree = table_ref.shape[3]
    steps = lax.broadcasted_iota(jnp.int32, (1, half_degree), 1)
    norm = float(trunc * (trunc + 1))
    even_rows, odd_rows = [], []
    for s in range(4):
        pair = []
        for p, source in enumerate((sym, anti)):
            table = table_ref[s, p]
            spec = jnp.dot(source[32 * s : 32 * s + 32], table, preferred_element_type=F32)
            degree = (waves_ref[first + s] + 2 * steps + p).astype(F32)
            divisor = 1.0 + gamma * (degree * (degree + 1.0)) / norm
            solved = (spec / divisor).astype(BF16)
            pair.append(
                4.0
                * lax.dot_general(
                    solved, table, (((1,), (1,)), ((), ())), preferred_element_type=F32
                )
            )
        even_rows.append(pair[0])
        odd_rows.append(pair[1])
    even = jnp.concatenate(even_rows, axis=0)
    odd = jnp.concatenate(odd_rows, axis=0)
    north = jnp.transpose(even + odd).astype(BF16)
    south = jnp.transpose(even - odd).astype(BF16)
    return north, permuted(turn, south).astype(BF16)


def departure_weights(start, row_ref, col_ref, rw_ref, cw_ref, near_ref, col_w_ref, far_ref):
    lon = row_ref.shape[1]
    sub = lax.broadcasted_iota(jnp.int32, (8, lon), 0) - 2
    lon_ids = lax.broadcasted_iota(jnp.int32, (1, lon), 1)
    for i in range(2):
        rel_row = row_ref[i : i + 1, :] - (start + i)
        rel_col = ((col_ref[i : i + 1, :] - lon_ids + 2) & (lon - 1)) - 2
        a = rw_ref[i : i + 1, :]
        b = cw_ref[i : i + 1, :]
        row_w = jnp.where(rel_row == sub, 1.0 - a, 0.0) + jnp.where(rel_row == sub - 1, a, 0.0)
        col_w = jnp.where(rel_col == sub, 1.0 - b, 0.0) + jnp.where(rel_col == sub - 1, b, 0.0)
        for dc in range(-2, 4):
            near_ref[i, dc + 2] = row_w if dc == 0 else pltpu.roll(row_w, dc % lon, 1)
        col_w_ref[i] = col_w
        far_ref[i] = row_w[4 * i : 4 * i + 1, :] * col_w


def near_rows(sources, near_ref, col_w_ref, departed_ref):
    levels, lon = departed_ref.shape[1:]
    for i in range(2):
        for h in range(levels // 8):
            total = None
            for dc in range(-2, 4):
                mixed = None
                for dr in range(1 - i, 5 - i):
                    term = (
                        near_ref[i, dc + 2, dr : dr + 1, :]
                        * sources[i + dr - 1, 8 * h : 8 * h + 8, :]
                    )
                    mixed = term if mixed is None else mixed + term
                if dc != 0:
                    mixed = pltpu.roll(mixed, (-dc) % lon, 1)
                term = col_w_ref[i, dc + 2 : dc + 3, :] * mixed
                total = term if total is None else total + term
            departed_ref[i, 8 * h : 8 * h + 8, :] = total


def far_rows(rows, far_ref, departed_ref):
    levels, lon = departed_ref.shape[1:]
    for i in range(2):
        for h in range(levels // 8):
            source = rows[i][8 * h : 8 * h + 8, :].astype(F32)
            total = departed_ref[i, 8 * h : 8 * h + 8, :]
            for dc in range(-2, 4):
                moved = source if dc == 0 else pltpu.roll(source, (-dc) % lon, 1)
                total = total + far_ref[i, dc + 2 : dc + 3, :] * moved
            departed_ref[i, 8 * h : 8 * h + 8, :] = total


def forward_waves(departed_ref, z_ref, tall_ref, fold, ft_ref, mix_ref, out_ref):
    levels, lon = departed_ref.shape[1:]
    for i in range(2):
        planes = [
            departed_ref[i, :, 128 * j : 128 * j + 128].astype(BF16).astype(F32)
            for j in range(RADIX)
        ]
        for k, (re, im) in enumerate(real_fft(planes)):
            at = 2 * levels * k + levels * i
            z_ref[at : at + levels, 0:128] = re.astype(BF16)
            z_ref[at : at + levels, 128:256] = (
                jnp.zeros((levels, 128), BF16) if im is None else im.astype(BF16)
            )
    scale = math.sqrt(2.0 / lon)
    r = 2 * levels
    for c in range(8):
        prod = jnp.dot(z_ref[...], tall_ref[c], preferred_element_type=F32)
        got = prod[0:r]
        for k in range(1, HALF):
            got = jnp.where(fold[c // 2] == k, prod[r * k : r * k + r], got)
        got = got * scale
        for i in range(2):
            ft_ref[128 * i + 16 * c : 128 * i + 16 * c + 16, :] = got[16 * i : 16 * i + 16]
    swapped = jnp.transpose(ft_ref[...])
    for i in range(2):
        mix_ref[pl.ds(i, 256, stride=2), :] = swapped[:, 128 * i : 128 * i + 128]
    out_ref[...] = mix_ref[...].astype(BF16).reshape(256, 2, 128)


def inverse_waves(got_ref, table_ref, fold, heat, e_ref, mix_ref, out_ref):
    levels, lon = out_ref.shape[1:]
    r = 2 * levels
    mix_ref[...] = got_ref[...].reshape(512, 128).astype(F32)
    turned = [jnp.transpose(mix_ref[pl.ds(i, 256, stride=2), :]) for i in range(2)]
    for c in range(8):
        piece = jnp.concatenate([t[16 * c : 16 * c + 16] for t in turned], axis=0)
        for k in range(HALF):
            e_ref[r * k : r * k + r, 256 * c : 256 * c + 256] = jnp.where(
                fold[c // 2] == k, piece, 0.0
            ).astype(BF16)
    waves = jnp.dot(e_ref[...], table_ref[...], preferred_element_type=F32)
    scale = 0.5 * math.sqrt(2.0 / lon)
    for i in range(2):
        spec = []
        for k in range(HALF):
            at = r * k + levels * i
            block = waves[at : at + levels]
            re, im = block[:, 0:128], block[:, 128:256]
            if k in (0, HALF - 1):
                spec.append((re + re, None))
            else:
                spec.append((re, im))
        for j, plane in enumerate(real_ifft(spec)):
            warm = heat[:, 128 * j : 128 * j + 128]
            out_ref[i, :, 128 * j : 128 * j + 128] = (plane * scale + warm).astype(BF16)


def coarse_means(own_ref):
    lon = own_ref.shape[2]
    high = lax.broadcasted_iota(jnp.int32, (512, 128), 0)
    low = lax.broadcasted_iota(jnp.int32, (512, 128), 1)
    pool = jnp.where(high // 4 == low, 1.0, 0.0).astype(BF16)
    temps = []
    for b in range(lon // 512):
        part = None
        for e in range(2):
            term = jnp.dot(
                own_ref[e, :, 512 * b : 512 * b + 512], pool, preferred_element_type=F32
            )
            part = term if part is None else part + term
        temps.append(part)
    return (jnp.concatenate(temps, axis=1) * 0.125).astype(BF16).astype(F32)


def radiate(temps, place, optics_ref, kabs, planck, kdown):
    levels, cols = temps.shape
    slot = place & (cols - 1)
    owner = place // cols
    block = (owner & 1) * 16 + owner // 2
    depth_all = None
    for b in range(cols // 256):
        ids = lax.broadcasted_iota(jnp.int32, (256, cols), 0) + 256 * b
        hot = jnp.where(ids == slot, 1.0, 0.0).astype(BF16)
        term = jnp.dot(
            optics_ref[:, 256 * b : 256 * b + 256], hot, preferred_element_type=F32
        )
        depth_all = term if depth_all is None else depth_all + term
    depth = depth_all[0:levels]
    for o in range(1, optics_ref.shape[0] // levels):
        depth = jnp.where(block == o, depth_all[levels * o : levels * o + levels], depth)
    best = lax.Precision.HIGHEST
    emission = 1.0 + jnp.tanh(temps)
    optical = jnp.dot(kabs, depth, precision=best, preferred_element_type=F32)
    source = jnp.dot(planck, emission, precision=best, preferred_element_type=F32)
    return jnp.dot(
        kdown, jnp.exp(-optical) * source, precision=best, preferred_element_type=F32
    ).astype(BF16)


def spread_heat(heat, lon):
    low = lax.broadcasted_iota(jnp.int32, (128, 512), 0)
    high = lax.broadcasted_iota(jnp.int32, (128, 512), 1)
    spread = jnp.where(low == high // 4, 1.0, 0.0).astype(BF16)
    return jnp.concatenate(
        [
            jnp.dot(heat[:, 128 * b : 128 * b + 128], spread, preferred_element_type=F32)
            for b in range(lon // 512)
        ],
        axis=1,
    )


def slot_waves(wave_tile):
    lane = lax.broadcasted_iota(jnp.int32, (128, 1024), 0)
    spot = lax.broadcasted_iota(jnp.int32, (128, 1024), 1)
    pick = jnp.where(lane == 4 * (spot & 31) + spot // 256, 1.0, 0.0).astype(BF16)
    high = (wave_tile // 32).astype(F32).astype(BF16)
    low = (wave_tile & 31).astype(F32).astype(BF16)
    spread = 32.0 * jnp.dot(high, pick, preferred_element_type=F32) + jnp.dot(
        low, pick, preferred_element_type=F32
    )
    group = lax.broadcasted_iota(jnp.int32, (8, 1024), 0)
    spot = lax.broadcasted_iota(jnp.int32, (8, 1024), 1)
    flat = jnp.sum(jnp.where(group == (spot & 255) // 32, spread, 0.0), axis=0, keepdims=True)
    return [flat[:, 256 * s : 256 * s + 256] for s in range(4)]


def turn_values(wave, step, lon):
    quarter = lon // 4
    point = (wave * step) & (lon - 1)
    turn = (point + quarter // 2) // quarter
    x = (point - turn * quarter).astype(F32) * (2.0 * math.pi / lon)
    y = x * x
    cosine = 1.0 + y * (-0.5 + y * (1.0 / 24 + y * (-1.0 / 720 + y * (1.0 / 40320))))
    sine = x * (1.0 + y * (-1.0 / 6 + y * (1.0 / 120 + y * (-1.0 / 5040 + y / 362880))))
    swap = (turn & 1) == 1
    c = jnp.where(swap, sine, cosine)
    n = jnp.where(swap, cosine, sine)
    c = jnp.where(((turn + 1) & 2) == 2, -c, c)
    n = jnp.where((turn & 2) == 2, -n, n)
    side = jnp.where((wave & (RADIX - 1)) > RADIX // 2, -1.0, 1.0)
    return c.astype(BF16), (side * n).astype(BF16), (-n).astype(BF16), (side * c).astype(BF16)


def fold_of(rows):
    fold = []
    for row in rows:
        kind = row.astype(jnp.int32) & (RADIX - 1)
        fold.append(jnp.minimum(kind, RADIX - kind))
    return fold


def tall_table(rows, tall_ref, lon):
    step = lax.broadcasted_iota(jnp.int32, (128, 256), 0)
    for s in range(4):
        a, b, c, d = turn_values(rows[s].astype(jnp.int32), step, lon)
        tall_ref[2 * s, 0:128, :] = a
        tall_ref[2 * s, 128:256, :] = b
        tall_ref[2 * s + 1, 0:128, :] = c
        tall_ref[2 * s + 1, 128:256, :] = d


def wide_table(rows, table_ref, lon):
    columns = jnp.transpose(jnp.concatenate(rows + [jnp.zeros((124, 256), F32)], axis=0))
    step = lax.broadcasted_iota(jnp.int32, (256, 128), 1)
    for s in range(4):
        a, b, c, d = turn_values(columns[:, s : s + 1].astype(jnp.int32), step, lon)
        at = 512 * s
        table_ref[at : at + 256, 0:128] = a
        table_ref[at : at + 256, 128:256] = b
        table_ref[at + 256 : at + 512, 0:128] = c
        table_ref[at + 256 : at + 512, 128:256] = d


def level_column(gamma_ref, rows):
    at = lax.broadcasted_iota(jnp.int32, (rows, 1), 0)
    levels = gamma_ref.shape[0]
    column = jnp.zeros((rows, 1), F32)
    for l in range(levels):
        column = jnp.where(at % levels == l, gamma_ref[l], column)
    return column


def tall(matrix):
    return jnp.transpose(jnp.concatenate([matrix, jnp.zeros((112, 128), F32)], axis=0))[:, 0:16]


def step_kernel(
    trunc, state_hbm, row_hbm, col_hbm, rw_hbm, cw_hbm, waves_ref, wave_tile_hbm, legendre_hbm,
    gamma_ref, place_hbm, optics_hbm, kabs_hbm, planck_hbm, kdown_hbm, out_ref,
    row_ref, col_ref, rw_ref, cw_ref, wave_tile_ref, legendre_ref, place_ref, optics_ref,
    kabs_ref, planck_ref, kdown_ref,
    raw_ref, own_ref, before, after, sources, near_ref, col_w_ref, far_ref, departed, table, tall_ref, z_ref, ft_ref, mix_ref, e_ref, optics_all,
    sent, got, answer, back,
    load_sems, halo_send, halo_recv, opt_send, opt_recv, relay_send, relay_recv,
    out_send, out_recv, back_send, back_recv, ready,
):
    g = lax.axis_index("grp")
    a = lax.axis_index("lat")
    me = g * 32 + a
    levels, lon = own_ref.shape[1:]
    moves = (
        (wave_tile_hbm, wave_tile_ref), (optics_hbm, optics_ref),
        (row_hbm, row_ref), (col_hbm, col_ref), (rw_hbm, rw_ref), (cw_hbm, cw_ref),
        (legendre_hbm, legendre_ref), (place_hbm, place_ref), (kabs_hbm, kabs_ref),
        (planck_hbm, planck_ref), (kdown_hbm, kdown_ref), (state_hbm, raw_ref),
    )
    loads = [
        pltpu.make_async_copy(src, dst, load_sems.at[n]) for n, (src, dst) in enumerate(moves)
    ]
    for load in loads[-1:] + loads[:-1]:
        load.start()

    barrier = pltpu.get_barrier_semaphore()
    following = lax.rem(me + 1, 256)
    previous = lax.rem(me + 255, 256)
    for other in (following, previous):
        pl.semaphore_signal(
            barrier, inc=1, device_id=(other // 32, lax.rem(other, 32)), device_id_type=MESH
        )

    @pl.loop(1, 32)
    def _(k):
        pl.semaphore_signal(
            barrier, inc=1, device_id=(g, lax.rem(a + k, 32)), device_id_type=MESH
        )

    @pl.loop(1, 8)
    def _(k):
        pl.semaphore_signal(
            barrier, inc=1, device_id=(lax.rem(g + k, 8), a), device_id_type=MESH
        )

    loads[-1].wait()
    for n in range(lon // 512):
        part = slice(512 * n, 512 * n + 512)
        block = raw_ref[:, :, part].astype(F32)
        for i in range(2):
            sources[1 + i, :, part] = block[:, i, :]
            own_ref[i, :, part] = block[:, i, :].astype(BF16)
    loads[0].wait()
    rows = slot_waves(wave_tile_ref[...])
    fold = fold_of(rows)
    tall_table(rows, tall_ref, lon)
    loads[1].wait()

    pl.semaphore_wait(barrier, 40)

    def halo(n, row):
        other, target = ((following, before), (previous, after))[n]
        return pltpu.make_async_remote_copy(
            src_ref=own_ref.at[row], dst_ref=target.at[row],
            send_sem=halo_send.at[2 * n + row], recv_sem=halo_recv.at[2 * n + row],
            device_id=(other // 32, lax.rem(other, 32)), device_id_type=MESH,
        )

    near = (halo(0, 1), halo(1, 0))
    far = (halo(0, 0), halo(1, 1))
    for move in near + far:
        move.start()

    @pl.loop(1, 8)
    def _(k):
        pl.semaphore_signal(
            ready, inc=1, device_id=(lax.rem(g + k, 8), a), device_id_type=MESH
        )

    core, chip = lax.rem(a, 2), a // 2

    def optics_rows(which):
        return pl.ds(pl.multiple_of((core * 16 + which) * levels, levels), levels)

    def optics_copy(k, peer, block):
        return pltpu.make_async_remote_copy(
            src_ref=optics_ref, dst_ref=optics_all.at[optics_rows(block)],
            send_sem=opt_send.at[k], recv_sem=opt_recv.at[k],
            device_id=(g, peer * 2 + core), device_id_type=MESH,
        )

    optics_all[optics_rows(chip), :] = optics_ref[...]
    temps = coarse_means(own_ref)
    wide_table(rows, table, lon)

    def exchange(source, target, send_sem, recv_sem):
        def send(z, lat):
            pltpu.make_async_remote_copy(
                src_ref=source.at[z * 32 + lat], dst_ref=target.at[me],
                send_sem=send_sem.at[0], recv_sem=recv_sem.at[0],
                device_id=(z, lat), device_id_type=MESH,
            ).start()

        @pl.loop(0, 7)
        def _(k):
            z = g ^ jnp.where(k < 4, 4 + k, 7 - k)
            for step in LAT_STEPS:
                send(z, a ^ step)

        for step in LAT_STEPS[:-1]:
            send(g, a ^ step)
        target[me] = source[me]
        return pltpu.make_async_remote_copy(
            src_ref=source.at[pl.ds(0, 255)], dst_ref=target.at[pl.ds(0, 255)],
            send_sem=send_sem.at[0], recv_sem=recv_sem.at[0],
            device_id=(lax.rem(g + 1, 8), a), device_id_type=MESH,
        )

    for load in loads[2:6]:
        load.wait()
    departure_weights(
        2 * me, row_ref, col_ref, rw_ref, cw_ref, near_ref, col_w_ref, far_ref
    )
    for move in near:
        move.wait_recv()
    sources[0] = before[1].astype(F32)
    sources[3] = after[0].astype(F32)
    near_rows(sources, near_ref, col_w_ref, departed)
    for move in far:
        move.wait_recv()

    @pl.loop(1, 16)
    def _(k):
        optics_copy(k, lax.rem(chip + k, 16), chip).start()

    far_rows((before.at[0], after.at[1]), far_ref, departed)
    forward_waves(departed, z_ref, tall_ref, fold, ft_ref, mix_ref, sent)
    pl.semaphore_wait(ready, 7)

    outward = exchange(sent, got, out_send, out_recv)

    @pl.loop(1, 16)
    def _(k):
        optics_copy(k, lax.rem(chip + k, 16), chip).wait_send()
        optics_copy(k, chip, lax.rem(chip + 16 - k, 16)).wait_recv()

    def relay_copy(which):
        half = optics_all.at[pl.ds(pl.multiple_of(which * (16 * levels), 16 * levels), 16 * levels)]
        return pltpu.make_async_remote_copy(
            src_ref=half, dst_ref=half, send_sem=relay_send.at[0], recv_sem=relay_recv.at[0],
            device_id=(g, chip * 2 + 1 - core), device_id_type=MESH,
        )

    relay_copy(core).start()
    turn = one_hot((256, 256), lambda row: 255 - row)
    gamma = level_column(gamma_ref, 2 * levels)
    loads[6].wait()
    outward.wait_recv()
    north, south = legendre_step(
        got[0:128].reshape(256, 128), got[128:256].reshape(256, 128), legendre_ref, gamma,
        waves_ref, me * 4, turn, trunc,
    )
    answer[0:128] = north.reshape(128, 2, 128)
    answer[128:256] = south.reshape(128, 2, 128)
    homeward = exchange(answer, back, back_send, back_recv)
    for load in loads[7:11]:
        load.wait()
    relay_copy(1 - core).wait_recv()
    heat = radiate(
        temps, place_ref[...], optics_all, tall(kabs_ref[...]), tall(planck_ref[...]),
        kdown_ref[...],
    )
    heat = spread_heat(heat, lon)
    homeward.wait_recv()
    inverse_waves(back, table, fold, heat, e_ref, mix_ref, out_ref)
    for move in near + far:
        move.wait_send()
    relay_copy(core).wait_send()
    outward.wait_send()
    homeward.wait_send()


def shards(
    state, dep_row, dep_col, row_weight, col_weight, wave_of, legendre, gamma,
    rad_place, optics, kabs, planck_weight, kdown,
):
    levels, lat_rows, lon = state.shape
    owners = lax.axis_size("lat")
    groups = lax.axis_size("grp")
    trunc = wave_of.shape[0] - 1
    coarse = lon // 4
    in_vmem = pl.BlockSpec(memory_space=pltpu.VMEM)
    in_smem = pl.BlockSpec(memory_space=pltpu.SMEM)
    in_hbm = pl.BlockSpec(memory_space=pltpu.HBM)
    dma = pltpu.SemaphoreType.DMA
    result = pl.pallas_call(
        functools.partial(step_kernel, trunc),
        out_shape=jax.ShapeDtypeStruct((lat_rows, levels, lon), BF16),
        in_specs=[
            in_hbm, in_hbm, in_hbm, in_hbm, in_hbm, in_smem, in_hbm, in_hbm,
            in_smem, in_hbm, in_hbm, in_hbm, in_hbm, in_hbm,
        ],
        out_specs=in_vmem,
        scratch_shapes=[
            pltpu.VMEM((lat_rows, lon), jnp.int32),
            pltpu.VMEM((lat_rows, lon), jnp.int32),
            pltpu.VMEM((lat_rows, lon), F32),
            pltpu.VMEM((lat_rows, lon), F32),
            pltpu.VMEM((groups, owners * 4), jnp.int32),
            pltpu.VMEM(legendre.shape, BF16),
            pltpu.VMEM((1, coarse), jnp.int32),
            pltpu.VMEM((levels, coarse), BF16),
            pltpu.VMEM((levels, 128), F32),
            pltpu.VMEM((levels, 128), F32),
            pltpu.VMEM((levels, 128), F32),
            pltpu.VMEM((levels, lat_rows, lon), BF16),
            pltpu.VMEM((lat_rows, levels, lon), BF16),
            pltpu.VMEM((lat_rows, levels, lon), BF16),
            pltpu.VMEM((lat_rows, levels, lon), BF16),
            pltpu.VMEM((4, levels, lon), F32),
            pltpu.VMEM((2, 6, 8, lon), F32),
            pltpu.VMEM((2, 8, lon), F32),
            pltpu.VMEM((2, 8, lon), F32),
            pltpu.VMEM((2, levels, lon), F32),
            pltpu.VMEM((2048, 256), BF16),
            pltpu.VMEM((8, 256, 256), BF16),
            pltpu.VMEM((HALF * 2 * levels, 256), BF16),
            pltpu.VMEM((256, 256), F32),
            pltpu.VMEM((512, 128), F32),
            pltpu.VMEM((HALF * 2 * levels, 2048), BF16),
            pltpu.VMEM((owners * levels, coarse), BF16),
        ]
        + [pltpu.VMEM((groups * owners, 2, 128), BF16)] * 4
        + [dma((12,)), dma((4,)), dma((4,)), dma((16,)), dma((16,)), dma((1,)), dma((1,))]
        + [dma((1,))] * 4
        + [pltpu.SemaphoreType.REGULAR],
        compiler_params=pltpu.CompilerParams(
            vmem_limit_bytes=VMEM_LIMIT, collective_id=0, has_side_effects=True
        ),
        name="model_step",
    )(
        state, dep_row, dep_col, row_weight, col_weight, wave_of,
        wave_of.reshape(groups, owners * 4), legendre, gamma, rad_place,
        jnp.transpose(optics), kabs, planck_weight, jnp.transpose(kdown),
    )
    return jnp.transpose(result, (1, 0, 2))


def solution(mesh):
    return jax.shard_map(
        shards,
        mesh=mesh,
        in_specs=(
            P(None, ("grp", "lat"), None),
            P(("grp", "lat"), None),
            P(("grp", "lat"), None),
            P(("grp", "lat"), None),
            P(("grp", "lat"), None),
            P(),
            P(("grp", "lat"), None, None, None),
            P(),
            P(("grp", "lat"), None),
            P(("grp", "lat"), None),
            P(),
            P(),
            P(),
        ),
        out_specs=P(None, ("grp", "lat"), None),
        check_vma=False,
    )
```

```python
import functools
import math

import jax
import jax.numpy as jnp
from jax import lax
from jax.experimental import pallas as pl
from jax.experimental.pallas import tpu as pltpu
from jax.sharding import PartitionSpec as P

F32 = jnp.float32
BF16 = jnp.bfloat16
RADIX = 32
HALF = RADIX // 2 + 1
VMEM_LIMIT = 62 * 1024 * 1024
MESH = pl.DeviceIdType.MESH
LAT_STEPS = [8 * y + 2 * x + c for y in (2, 1, 3, 0) for x in (2, 1, 3, 0) for c in (1, 0)]


def cplx(angle_num, angle_den):
    turn = 2.0 * math.pi * angle_num / angle_den
    return math.cos(turn), math.sin(turn)


def real_fft(planes):
    count = len(planes)
    if count == 2:
        return [(planes[0] + planes[1], None), (planes[0] - planes[1], None)]
    even = real_fft(planes[0::2])
    odd = real_fft(planes[1::2])
    half = count // 2
    out = []
    for k in range(half + 1):

        def pick(spec):
            kk = k % half
            if kk <= half // 2:
                return spec[kk]
            re, im = spec[half - kk]
            return re, (None if im is None else -im)

        er, ei = pick(even)
        orr, oi = pick(odd)
        c, s = cplx(k, count)
        if k == 0:
            out.append((er + orr, None))
        elif k == half:
            out.append((er - orr, None))
        elif 4 * k == count:
            out.append((er, -orr))
        else:
            if oi is None:
                tr, ti = c * orr, -s * orr
            else:
                tr, ti = c * orr + s * oi, c * oi - s * orr
            out.append((er + tr, ti if ei is None else ei + ti))
    return out


def real_ifft(spec):
    half = len(spec) - 1
    count = 2 * half
    if count == 2:
        return [spec[0][0] + spec[1][0], spec[0][0] - spec[1][0]]
    even, odd = [], []
    for k in range(half // 2 + 1):
        xr, xi = spec[k]
        yr, yi = spec[half - k]
        if k == 0:
            even.append((xr + yr, None))
            odd.append((xr - yr, None))
        elif 2 * k == half:
            even.append((xr + xr, None))
            odd.append((-(xi + xi), None))
        else:
            even.append((xr + yr, xi - yi))
            dr, di = xr - yr, xi + yi
            c, s = cplx(k, count)
            odd.append((c * dr - s * di, c * di + s * dr))
    ev, od = real_ifft(even), real_ifft(odd)
    return [plane for pair in zip(ev, od) for plane in pair]


def one_hot(shape, want):
    rows = lax.broadcasted_iota(jnp.int32, shape, 0)
    cols = lax.broadcasted_iota(jnp.int32, shape, 1)
    return jnp.where(want(rows) == cols, 1.0, 0.0).astype(BF16)


def permuted(matrix, data):
    return jnp.dot(matrix, data, preferred_element_type=F32)


def legendre_step(north_in, south_in, table_ref, gamma, waves_ref, first, turn, trunc):
    north = north_in.astype(F32)
    south = permuted(turn, south_in)
    sym = jnp.transpose(north + south).astype(BF16)
    anti = jnp.transpose(north - south).astype(BF16)
    half_degree = table_ref.shape[3]
    steps = lax.broadcasted_iota(jnp.int32, (1, half_degree), 1)
    norm = float(trunc * (trunc + 1))
    even_rows, odd_rows = [], []
    for s in range(4):
        pair = []
        for p, source in enumerate((sym, anti)):
            table = table_ref[s, p]
            spec = jnp.dot(source[32 * s : 32 * s + 32], table, preferred_element_type=F32)
            degree = (waves_ref[first + s] + 2 * steps + p).astype(F32)
            divisor = 1.0 + gamma * (degree * (degree + 1.0)) / norm
            solved = (spec / divisor).astype(BF16)
            pair.append(
                4.0
                * lax.dot_general(
                    solved, table, (((1,), (1,)), ((), ())), preferred_element_type=F32
                )
            )
        even_rows.append(pair[0])
        odd_rows.append(pair[1])
    even = jnp.concatenate(even_rows, axis=0)
    odd = jnp.concatenate(odd_rows, axis=0)
    north = jnp.transpose(even + odd).astype(BF16)
    south = jnp.transpose(even - odd).astype(BF16)
    return north, permuted(turn, south).astype(BF16)


def departure_weights(start, row_ref, col_ref, rw_ref, cw_ref, near_ref, col_w_ref, far_ref):
    lon = row_ref.shape[1]
    sub = lax.broadcasted_iota(jnp.int32, (8, lon), 0) - 2
    lon_ids = lax.broadcasted_iota(jnp.int32, (1, lon), 1)
    for i in range(2):
        rel_row = row_ref[i : i + 1, :] - (start + i)
        rel_col = ((col_ref[i : i + 1, :] - lon_ids + 2) & (lon - 1)) - 2
        a = rw_ref[i : i + 1, :]
        b = cw_ref[i : i + 1, :]
        row_w = jnp.where(rel_row == sub, 1.0 - a, 0.0) + jnp.where(rel_row == sub - 1, a, 0.0)
        col_w = jnp.where(rel_col == sub, 1.0 - b, 0.0) + jnp.where(rel_col == sub - 1, b, 0.0)
        for dc in range(-2, 4):
            near_ref[i, dc + 2] = row_w if dc == 0 else pltpu.roll(row_w, dc % lon, 1)
        col_w_ref[i] = col_w
        far_ref[i] = row_w[4 * i : 4 * i + 1, :] * col_w


def near_rows(sources, near_ref, col_w_ref, departed_ref):
    levels, lon = departed_ref.shape[1:]
    for i in range(2):
        for h in range(levels // 8):
            total = None
            for dc in range(-2, 4):
                mixed = None
                for dr in range(1 - i, 5 - i):
                    term = (
                        near_ref[i, dc + 2, dr : dr + 1, :]
                        * sources[i + dr - 1, 8 * h : 8 * h + 8, :]
                    )
                    mixed = term if mixed is None else mixed + term
                if dc != 0:
                    mixed = pltpu.roll(mixed, (-dc) % lon, 1)
                term = col_w_ref[i, dc + 2 : dc + 3, :] * mixed
                total = term if total is None else total + term
            departed_ref[i, 8 * h : 8 * h + 8, :] = total


def far_rows(rows, far_ref, departed_ref):
    levels, lon = departed_ref.shape[1:]
    for i in range(2):
        for h in range(levels // 8):
            source = rows[i][8 * h : 8 * h + 8, :].astype(F32)
            total = departed_ref[i, 8 * h : 8 * h + 8, :]
            for dc in range(-2, 4):
                moved = source if dc == 0 else pltpu.roll(source, (-dc) % lon, 1)
                total = total + far_ref[i, dc + 2 : dc + 3, :] * moved
            departed_ref[i, 8 * h : 8 * h + 8, :] = total


def forward_waves(departed_ref, z_ref, tall_ref, fold, ft_ref, mix_ref, out_ref):
    levels, lon = departed_ref.shape[1:]
    for i in range(2):
        planes = [
            departed_ref[i, :, 128 * j : 128 * j + 128].astype(BF16).astype(F32)
            for j in range(RADIX)
        ]
        for k, (re, im) in enumerate(real_fft(planes)):
            at = 2 * levels * k + levels * i
            z_ref[at : at + levels, 0:128] = re.astype(BF16)
            z_ref[at : at + levels, 128:256] = (
                jnp.zeros((levels, 128), BF16) if im is None else im.astype(BF16)
            )
    scale = math.sqrt(2.0 / lon)
    r = 2 * levels
    for c in range(8):
        prod = jnp.dot(z_ref[...], tall_ref[c], preferred_element_type=F32)
        got = prod[0:r]
        for k in range(1, HALF):
            got = jnp.where(fold[c // 2] == k, prod[r * k : r * k + r], got)
        got = got * scale
        for i in range(2):
            ft_ref[128 * i + 16 * c : 128 * i + 16 * c + 16, :] = got[16 * i : 16 * i + 16]
    swapped = jnp.transpose(ft_ref[...])
    for i in range(2):
        mix_ref[pl.ds(i, 256, stride=2), :] = swapped[:, 128 * i : 128 * i + 128]
    out_ref[...] = mix_ref[...].astype(BF16).reshape(256, 2, 128)


def inverse_waves(got_ref, table_ref, fold, heat, e_ref, mix_ref, out_ref):
    levels, lon = out_ref.shape[1:]
    r = 2 * levels
    mix_ref[...] = got_ref[...].reshape(512, 128).astype(F32)
    turned = [jnp.transpose(mix_ref[pl.ds(i, 256, stride=2), :]) for i in range(2)]
    for c in range(8):
        piece = jnp.concatenate([t[16 * c : 16 * c + 16] for t in turned], axis=0)
        for k in range(HALF):
            e_ref[r * k : r * k + r, 256 * c : 256 * c + 256] = jnp.where(
                fold[c // 2] == k, piece, 0.0
            ).astype(BF16)
    waves = jnp.dot(e_ref[...], table_ref[...], preferred_element_type=F32)
    scale = 0.5 * math.sqrt(2.0 / lon)
    for i in range(2):
        spec = []
        for k in range(HALF):
            at = r * k + levels * i
            block = waves[at : at + levels]
            re, im = block[:, 0:128], block[:, 128:256]
            if k in (0, HALF - 1):
                spec.append((re + re, None))
            else:
                spec.append((re, im))
        for j, plane in enumerate(real_ifft(spec)):
            warm = heat[:, 128 * j : 128 * j + 128]
            out_ref[i, :, 128 * j : 128 * j + 128] = (plane * scale + warm).astype(BF16)


def coarse_means(own_ref):
    lon = own_ref.shape[2]
    high = lax.broadcasted_iota(jnp.int32, (512, 128), 0)
    low = lax.broadcasted_iota(jnp.int32, (512, 128), 1)
    pool = jnp.where(high // 4 == low, 1.0, 0.0).astype(BF16)
    temps = []
    for b in range(lon // 512):
        part = None
        for e in range(2):
            term = jnp.dot(
                own_ref[e, :, 512 * b : 512 * b + 512], pool, preferred_element_type=F32
            )
            part = term if part is None else part + term
        temps.append(part)
    return (jnp.concatenate(temps, axis=1) * 0.125).astype(BF16).astype(F32)


def radiate(temps, place, optics_ref, kabs, planck, kdown):
    levels, cols = temps.shape
    slot = place & (cols - 1)
    owner = place // cols
    block = (owner & 1) * 16 + owner // 2
    depth_all = None
    for b in range(cols // 256):
        ids = lax.broadcasted_iota(jnp.int32, (256, cols), 0) + 256 * b
        hot = jnp.where(ids == slot, 1.0, 0.0).astype(BF16)
        term = jnp.dot(
            optics_ref[:, 256 * b : 256 * b + 256], hot, preferred_element_type=F32
        )
        depth_all = term if depth_all is None else depth_all + term
    depth = depth_all[0:levels]
    for o in range(1, optics_ref.shape[0] // levels):
        depth = jnp.where(block == o, depth_all[levels * o : levels * o + levels], depth)
    best = lax.Precision.HIGHEST
    emission = 1.0 + jnp.tanh(temps)
    optical = jnp.dot(kabs, depth, precision=best, preferred_element_type=F32)
    source = jnp.dot(planck, emission, precision=best, preferred_element_type=F32)
    return jnp.dot(
        kdown, jnp.exp(-optical) * source, precision=best, preferred_element_type=F32
    ).astype(BF16)


def spread_heat(heat, lon):
    low = lax.broadcasted_iota(jnp.int32, (128, 512), 0)
    high = lax.broadcasted_iota(jnp.int32, (128, 512), 1)
    spread = jnp.where(low == high // 4, 1.0, 0.0).astype(BF16)
    return jnp.concatenate(
        [
            jnp.dot(heat[:, 128 * b : 128 * b + 128], spread, preferred_element_type=F32)
            for b in range(lon // 512)
        ],
        axis=1,
    )


def slot_waves(wave_tile):
    lane = lax.broadcasted_iota(jnp.int32, (128, 1024), 0)
    spot = lax.broadcasted_iota(jnp.int32, (128, 1024), 1)
    pick = jnp.where(lane == 4 * (spot & 31) + spot // 256, 1.0, 0.0).astype(BF16)
    high = (wave_tile // 32).astype(F32).astype(BF16)
    low = (wave_tile & 31).astype(F32).astype(BF16)
    spread = 32.0 * jnp.dot(high, pick, preferred_element_type=F32) + jnp.dot(
        low, pick, preferred_element_type=F32
    )
    group = lax.broadcasted_iota(jnp.int32, (8, 1024), 0)
    spot = lax.broadcasted_iota(jnp.int32, (8, 1024), 1)
    flat = jnp.sum(jnp.where(group == (spot & 255) // 32, spread, 0.0), axis=0, keepdims=True)
    return [flat[:, 256 * s : 256 * s + 256] for s in range(4)]


def turn_values(wave, step, lon):
    quarter = lon // 4
    point = (wave * step) & (lon - 1)
    turn = (point + quarter // 2) // quarter
    x = (point - turn * quarter).astype(F32) * (2.0 * math.pi / lon)
    y = x * x
    cosine = 1.0 + y * (-0.5 + y * (1.0 / 24 + y * (-1.0 / 720 + y * (1.0 / 40320))))
    sine = x * (1.0 + y * (-1.0 / 6 + y * (1.0 / 120 + y * (-1.0 / 5040 + y / 362880))))
    swap = (turn & 1) == 1
    c = jnp.where(swap, sine, cosine)
    n = jnp.where(swap, cosine, sine)
    c = jnp.where(((turn + 1) & 2) == 2, -c, c)
    n = jnp.where((turn & 2) == 2, -n, n)
    side = jnp.where((wave & (RADIX - 1)) > RADIX // 2, -1.0, 1.0)
    return c.astype(BF16), (side * n).astype(BF16), (-n).astype(BF16), (side * c).astype(BF16)


def fold_of(rows):
    fold = []
    for row in rows:
        kind = row.astype(jnp.int32) & (RADIX - 1)
        fold.append(jnp.minimum(kind, RADIX - kind))
    return fold


def tall_table(rows, tall_ref, lon):
    step = lax.broadcasted_iota(jnp.int32, (128, 256), 0)
    for s in range(4):
        a, b, c, d = turn_values(rows[s].astype(jnp.int32), step, lon)
        tall_ref[2 * s, 0:128, :] = a
        tall_ref[2 * s, 128:256, :] = b
        tall_ref[2 * s + 1, 0:128, :] = c
        tall_ref[2 * s + 1, 128:256, :] = d


def wide_table(rows, table_ref, lon):
    columns = jnp.transpose(jnp.concatenate(rows + [jnp.zeros((124, 256), F32)], axis=0))
    step = lax.broadcasted_iota(jnp.int32, (256, 128), 1)
    for s in range(4):
        a, b, c, d = turn_values(columns[:, s : s + 1].astype(jnp.int32), step, lon)
        at = 512 * s
        table_ref[at : at + 256, 0:128] = a
        table_ref[at : at + 256, 128:256] = b
        table_ref[at + 256 : at + 512, 0:128] = c
        table_ref[at + 256 : at + 512, 128:256] = d


def level_column(gamma_ref, rows):
    at = lax.broadcasted_iota(jnp.int32, (rows, 1), 0)
    levels = gamma_ref.shape[0]
    column = jnp.zeros((rows, 1), F32)
    for l in range(levels):
        column = jnp.where(at % levels == l, gamma_ref[l], column)
    return column


def tall(matrix):
    return jnp.transpose(jnp.concatenate([matrix, jnp.zeros((112, 128), F32)], axis=0))[:, 0:16]


def step_kernel(
    trunc, state_hbm, row_hbm, col_hbm, rw_hbm, cw_hbm, waves_ref, wave_tile_hbm, legendre_hbm,
    gamma_ref, place_hbm, optics_hbm, kabs_hbm, planck_hbm, kdown_hbm, out_ref,
    row_ref, col_ref, rw_ref, cw_ref, wave_tile_ref, legendre_ref, place_ref, optics_ref,
    kabs_ref, planck_ref, kdown_ref,
    raw_ref, own_ref, before, after, sources, near_ref, col_w_ref, far_ref, departed, table, tall_ref, z_ref, ft_ref, mix_ref, e_ref, optics_all,
    sent, got, answer, back,
    load_sems, halo_send, halo_recv, opt_send, opt_recv, relay_send, relay_recv,
    out_send, out_recv, back_send, back_recv, ready,
):
    g = lax.axis_index("grp")
    a = lax.axis_index("lat")
    me = g * 32 + a
    levels, lon = own_ref.shape[1:]
    moves = (
        (wave_tile_hbm, wave_tile_ref), (optics_hbm, optics_ref),
        (row_hbm, row_ref), (col_hbm, col_ref), (rw_hbm, rw_ref), (cw_hbm, cw_ref),
        (legendre_hbm, legendre_ref), (place_hbm, place_ref), (kabs_hbm, kabs_ref),
        (planck_hbm, planck_ref), (kdown_hbm, kdown_ref), (state_hbm, raw_ref),
    )
    loads = [
        pltpu.make_async_copy(src, dst, load_sems.at[n]) for n, (src, dst) in enumerate(moves)
    ]
    for load in loads[-1:] + loads[:-1]:
        load.start()

    barrier = pltpu.get_barrier_semaphore()
    following = lax.rem(me + 1, 256)
    previous = lax.rem(me + 255, 256)
    for other in (following, previous):
        pl.semaphore_signal(
            barrier, inc=1, device_id=(other // 32, lax.rem(other, 32)), device_id_type=MESH
        )

    @pl.loop(1, 32)
    def _(k):
        pl.semaphore_signal(
            barrier, inc=1, device_id=(g, lax.rem(a + k, 32)), device_id_type=MESH
        )

    @pl.loop(1, 8)
    def _(k):
        pl.semaphore_signal(
            barrier, inc=1, device_id=(lax.rem(g + k, 8), a), device_id_type=MESH
        )

    loads[-1].wait()
    for n in range(lon // 512):
        part = slice(512 * n, 512 * n + 512)
        block = raw_ref[:, :, part].astype(F32)
        for i in range(2):
            sources[1 + i, :, part] = block[:, i, :]
            own_ref[i, :, part] = block[:, i, :].astype(BF16)
    loads[0].wait()
    rows = slot_waves(wave_tile_ref[...])
    fold = fold_of(rows)
    tall_table(rows, tall_ref, lon)
    loads[1].wait()

    pl.semaphore_wait(barrier, 40)

    def halo(n, row):
        other, target = ((following, before), (previous, after))[n]
        return pltpu.make_async_remote_copy(
            src_ref=own_ref.at[row], dst_ref=target.at[row],
            send_sem=halo_send.at[2 * n + row], recv_sem=halo_recv.at[2 * n + row],
            device_id=(other // 32, lax.rem(other, 32)), device_id_type=MESH,
        )

    near = (halo(0, 1), halo(1, 0))
    far = (halo(0, 0), halo(1, 1))
    for move in near + far:
        move.start()

    @pl.loop(1, 8)
    def _(k):
        pl.semaphore_signal(
            ready, inc=1, device_id=(lax.rem(g + k, 8), a), device_id_type=MESH
        )

    core, chip = lax.rem(a, 2), a // 2

    def optics_rows(which):
        return pl.ds(pl.multiple_of((core * 16 + which) * levels, levels), levels)

    def optics_copy(k, peer, block):
        return pltpu.make_async_remote_copy(
            src_ref=optics_ref, dst_ref=optics_all.at[optics_rows(block)],
            send_sem=opt_send.at[k], recv_sem=opt_recv.at[k],
            device_id=(g, peer * 2 + core), device_id_type=MESH,
        )

    optics_all[optics_rows(chip), :] = optics_ref[...]
    temps = coarse_means(own_ref)
    wide_table(rows, table, lon)

    def exchange(source, target, send_sem, recv_sem):
        def send(z, lat):
            pltpu.make_async_remote_copy(
                src_ref=source.at[z * 32 + lat], dst_ref=target.at[me],
                send_sem=send_sem.at[0], recv_sem=recv_sem.at[0],
                device_id=(z, lat), device_id_type=MESH,
            ).start()

        @pl.loop(0, 7)
        def _(k):
            z = g ^ jnp.where(k < 2, 4 + k, jnp.where(k == 2, 3, jnp.where(k < 5, 10 - k, 7 - k)))
            for step in LAT_STEPS:
                send(z, a ^ step)

        for step in LAT_STEPS[:-1]:
            send(g, a ^ step)
        target[me] = source[me]
        return pltpu.make_async_remote_copy(
            src_ref=source.at[pl.ds(0, 255)], dst_ref=target.at[pl.ds(0, 255)],
            send_sem=send_sem.at[0], recv_sem=recv_sem.at[0],
            device_id=(lax.rem(g + 1, 8), a), device_id_type=MESH,
        )

    for load in loads[2:6]:
        load.wait()
    departure_weights(
        2 * me, row_ref, col_ref, rw_ref, cw_ref, near_ref, col_w_ref, far_ref
    )
    for move in near:
        move.wait_recv()
    sources[0] = before[1].astype(F32)
    sources[3] = after[0].astype(F32)
    near_rows(sources, near_ref, col_w_ref, departed)
    for move in far:
        move.wait_recv()

    @pl.loop(1, 16)
    def _(k):
        optics_copy(k, lax.rem(chip + k, 16), chip).start()

    far_rows((before.at[0], after.at[1]), far_ref, departed)
    forward_waves(departed, z_ref, tall_ref, fold, ft_ref, mix_ref, sent)
    pl.semaphore_wait(ready, 7)

    outward = exchange(sent, got, out_send, out_recv)

    @pl.loop(1, 16)
    def _(k):
        optics_copy(k, lax.rem(chip + k, 16), chip).wait_send()
        optics_copy(k, chip, lax.rem(chip + 16 - k, 16)).wait_recv()

    def relay_copy(which):
        half = optics_all.at[pl.ds(pl.multiple_of(which * (16 * levels), 16 * levels), 16 * levels)]
        return pltpu.make_async_remote_copy(
            src_ref=half, dst_ref=half, send_sem=relay_send.at[0], recv_sem=relay_recv.at[0],
            device_id=(g, chip * 2 + 1 - core), device_id_type=MESH,
        )

    relay_copy(core).start()
    turn = one_hot((256, 256), lambda row: 255 - row)
    gamma = level_column(gamma_ref, 2 * levels)
    loads[6].wait()
    outward.wait_recv()
    north, south = legendre_step(
        got[0:128].reshape(256, 128), got[128:256].reshape(256, 128), legendre_ref, gamma,
        waves_ref, me * 4, turn, trunc,
    )
    answer[0:128] = north.reshape(128, 2, 128)
    answer[128:256] = south.reshape(128, 2, 128)
    homeward = exchange(answer, back, back_send, back_recv)
    for load in loads[7:11]:
        load.wait()
    relay_copy(1 - core).wait_recv()
    heat = radiate(
        temps, place_ref[...], optics_all, tall(kabs_ref[...]), tall(planck_ref[...]),
        kdown_ref[...],
    )
    heat = spread_heat(heat, lon)
    homeward.wait_recv()
    inverse_waves(back, table, fold, heat, e_ref, mix_ref, out_ref)
    for move in near + far:
        move.wait_send()
    relay_copy(core).wait_send()
    outward.wait_send()
    homeward.wait_send()


def shards(
    state, dep_row, dep_col, row_weight, col_weight, wave_of, legendre, gamma,
    rad_place, optics, kabs, planck_weight, kdown,
):
    levels, lat_rows, lon = state.shape
    owners = lax.axis_size("lat")
    groups = lax.axis_size("grp")
    trunc = wave_of.shape[0] - 1
    coarse = lon // 4
    in_vmem = pl.BlockSpec(memory_space=pltpu.VMEM)
    in_smem = pl.BlockSpec(memory_space=pltpu.SMEM)
    in_hbm = pl.BlockSpec(memory_space=pltpu.HBM)
    dma = pltpu.SemaphoreType.DMA
    result = pl.pallas_call(
        functools.partial(step_kernel, trunc),
        out_shape=jax.ShapeDtypeStruct((lat_rows, levels, lon), BF16),
        in_specs=[
            in_hbm, in_hbm, in_hbm, in_hbm, in_hbm, in_smem, in_hbm, in_hbm,
            in_smem, in_hbm, in_hbm, in_hbm, in_hbm, in_hbm,
        ],
        out_specs=in_vmem,
        scratch_shapes=[
            pltpu.VMEM((lat_rows, lon), jnp.int32),
            pltpu.VMEM((lat_rows, lon), jnp.int32),
            pltpu.VMEM((lat_rows, lon), F32),
            pltpu.VMEM((lat_rows, lon), F32),
            pltpu.VMEM((groups, owners * 4), jnp.int32),
            pltpu.VMEM(legendre.shape, BF16),
            pltpu.VMEM((1, coarse), jnp.int32),
            pltpu.VMEM((levels, coarse), BF16),
            pltpu.VMEM((levels, 128), F32),
            pltpu.VMEM((levels, 128), F32),
            pltpu.VMEM((levels, 128), F32),
            pltpu.VMEM((levels, lat_rows, lon), BF16),
            pltpu.VMEM((lat_rows, levels, lon), BF16),
            pltpu.VMEM((lat_rows, levels, lon), BF16),
            pltpu.VMEM((lat_rows, levels, lon), BF16),
            pltpu.VMEM((4, levels, lon), F32),
            pltpu.VMEM((2, 6, 8, lon), F32),
            pltpu.VMEM((2, 8, lon), F32),
            pltpu.VMEM((2, 8, lon), F32),
            pltpu.VMEM((2, levels, lon), F32),
            pltpu.VMEM((2048, 256), BF16),
            pltpu.VMEM((8, 256, 256), BF16),
            pltpu.VMEM((HALF * 2 * levels, 256), BF16),
            pltpu.VMEM((256, 256), F32),
            pltpu.VMEM((512, 128), F32),
            pltpu.VMEM((HALF * 2 * levels, 2048), BF16),
            pltpu.VMEM((owners * levels, coarse), BF16),
        ]
        + [pltpu.VMEM((groups * owners, 2, 128), BF16)] * 4
        + [dma((12,)), dma((4,)), dma((4,)), dma((16,)), dma((16,)), dma((1,)), dma((1,))]
        + [dma((1,))] * 4
        + [pltpu.SemaphoreType.REGULAR],
        compiler_params=pltpu.CompilerParams(
            vmem_limit_bytes=VMEM_LIMIT, collective_id=0, has_side_effects=True
        ),
        name="model_step",
    )(
        state, dep_row, dep_col, row_weight, col_weight, wave_of,
        wave_of.reshape(groups, owners * 4), legendre, gamma, rad_place,
        jnp.transpose(optics), kabs, planck_weight, jnp.transpose(kdown),
    )
    return jnp.transpose(result, (1, 0, 2))


def solution(mesh):
    return jax.shard_map(
        shards,
        mesh=mesh,
        in_specs=(
            P(None, ("grp", "lat"), None),
            P(("grp", "lat"), None),
            P(("grp", "lat"), None),
            P(("grp", "lat"), None),
            P(("grp", "lat"), None),
            P(),
            P(("grp", "lat"), None, None, None),
            P(),
            P(("grp", "lat"), None),
            P(("grp", "lat"), None),
            P(),
            P(),
            P(),
        ),
        out_specs=P(None, ("grp", "lat"), None),
        check_vma=False,
    )
```
